256 devices in a mesh: seq: 128 (over x, z, y), rows: 2 (over core).
Axes of the slice: x: 4, y: 4, z: 8, core: 2. Of those that a mesh axis runs over, the one named last changes fastest.
Arguments:
- queries: bfloat16 [2, 8, 8192], P(None, None, 'seq'), may hold values from -6 to 6
- new_keys: bfloat16 [2, 8, 1024], P(None, None, 'seq'), may hold values from -16 to 16
- new_values: bfloat16 [2, 8, 1024], P(None, None, 'seq'), may hold values from -6 to 6
- key_cache: bfloat16 [8, 32768, 1024], P('rows', 'seq'), may hold values from -16 to 16
- value_cache: bfloat16 [8, 32768, 1024], P('rows', 'seq'), may hold values from -6 to 6
- lengths: int32 [8], replicated, may hold values from 2 to 32766, as said below
- row_slot: int32 [8], replicated, may hold values from 0 to 7, each once
Outputs:
- attended: bfloat16 [2, 8, 8192], P(None, None, 'seq')
The draws below stay inside these ranges and needn't reach their ends.
Inputs may be any that keep to these rules, and one draw needn't show every extreme that they name: `lengths`: every request has at least two cached tokens and room for 2 more; some request has exactly 32766.
All inputs are finite; a program needn't handle non-finite values.
Results may differ from the reference program's by a relative error of at most 0.0085.
Values may be sent and summed in bfloat16 or wider, within the bound.
A program may use at most 192 MiB of HBM per device.

```python
import jax
import jax.numpy as jnp
from jax import lax

Q_HEADS = 64
KV_HEADS = 8
HEAD_DIM = 128
STEPS = 2
ROWS = 8
CTX = 32768


def draw_lengths(key, part):
    key = jax.random.fold_in(key, 11)
    first, second = jax.random.split(key)
    drawn = jax.random.randint(first, (ROWS,), 2, CTX - 1, dtype=jnp.int32)
    longest = jax.random.randint(second, (), 0, ROWS, dtype=jnp.int32)
    marker = jnp.arange(ROWS, dtype=jnp.int32) == longest
    return jnp.where(marker, jnp.int32(CTX - 2), drawn)


def draw_queries(key, part):
    key = jax.random.fold_in(key, 21)
    drawn = jax.random.truncated_normal(key, -6.0, 6.0, (STEPS, ROWS, Q_HEADS, HEAD_DIM), jnp.float32)
    return drawn.reshape(STEPS, ROWS, Q_HEADS * HEAD_DIM).astype(jnp.bfloat16)


def draw_key_cache(key, part):
    key = jax.random.fold_in(key, 31)
    drawn = 3.0 * jax.random.truncated_normal(key, -16.0 / 3.0, 16.0 / 3.0, (ROWS, CTX, KV_HEADS, HEAD_DIM), jnp.float32)
    return drawn.reshape(ROWS, CTX, KV_HEADS * HEAD_DIM).astype(jnp.bfloat16)


def level_of(key, shape, shards, least, high):
    factor_of, own = 1.0, jax.random.fold_in(key, 6)
    for axis_at, blocks in shards:
        draws = jnp.exp(jax.random.uniform(jax.random.fold_in(own, axis_at), (blocks,), jnp.float32, least / len(shards), high / len(shards)))
        factor_of = factor_of * jnp.repeat(draws, shape[axis_at] // blocks).reshape([-1 if axis == axis_at else 1 for axis in range(len(shape))])
    return factor_of


def scatter_about(rng, extent, width, most, shards=(), kind=jnp.bfloat16):
    factor_of = level_of(rng, extent, shards, -0.22, 0.18) if shards else 1.0
    entries = jax.random.normal(rng, extent, jnp.float32) * width * factor_of
    return jnp.minimum(jnp.maximum(entries, -most), most).astype(kind)


def setup_inputs(seed: int = 0) -> dict:
    arg_keys = jax.random.split(jax.random.key(seed), 8)
    queries = draw_queries(jax.random.fold_in(arg_keys[7], 71), 0)
    new_keys = scatter_about(arg_keys[1], (STEPS, ROWS, KV_HEADS * HEAD_DIM), 3.0, 16.0, ((2, 128),))
    new_values = scatter_about(arg_keys[2], (STEPS, ROWS, KV_HEADS * HEAD_DIM), 1.0, 6.0, ((2, 128),))
    key_cache = draw_key_cache(jax.random.fold_in(arg_keys[7], 71), 0)
    value_cache = scatter_about(arg_keys[4], (ROWS, CTX, KV_HEADS * HEAD_DIM), 1.0, 6.0, ((0, 2), (1, 128)))
    lengths = draw_lengths(jax.random.fold_in(arg_keys[7], 71), 0)
    row_slot = jax.random.permutation(arg_keys[6], ROWS).astype(jnp.int32)
    return {"queries": queries, "new_keys": new_keys, "new_values": new_values, "key_cache": key_cache, "value_cache": value_cache, "lengths": lengths, "row_slot": row_slot}


def reference(queries, new_keys, new_values, key_cache, value_cache, lengths, row_slot):
    context = key_cache.shape[1]
    positions = jnp.arange(context, dtype=jnp.int32)
    group = Q_HEADS // KV_HEADS
    scale = HEAD_DIM ** -0.5

    def one_row(request):
        slot = row_slot[request]
        length = lengths[request]
        keys = key_cache[slot].astype(jnp.float32)
        values = value_cache[slot].astype(jnp.float32)
        for step in range(STEPS):
            hit = (positions == length + step)[:, None]
            keys = jnp.where(hit, new_keys[step, request].astype(jnp.float32)[None, :], keys)
            values = jnp.where(hit, new_values[step, request].astype(jnp.float32)[None, :], values)
        keys = keys.reshape(context, KV_HEADS, HEAD_DIM)
        values = values.reshape(context, KV_HEADS, HEAD_DIM)
        query = queries[:, request].astype(jnp.float32).reshape(STEPS, KV_HEADS, group, HEAD_DIM)
        scores = jnp.einsum("tkgd,nkd->tkgn", query, keys, precision=lax.Precision.HIGHEST) * scale
        limit = length + 1 + jnp.arange(STEPS, dtype=jnp.int32)
        valid = (positions[None, :] < limit[:, None])[:, None, None, :]
        masked = jnp.where(valid, scores, jnp.float32(-1e30))
        top = jnp.max(masked, axis=-1, keepdims=True)
        expo = jnp.where(valid, jnp.exp(masked - top), jnp.float32(0.0))
        weights = expo / jnp.sum(expo, axis=-1, keepdims=True)
        result = jnp.einsum("tkgn,nkd->tkgd", weights, values, precision=lax.Precision.HIGHEST)
        return result.reshape(STEPS, Q_HEADS * HEAD_DIM)

    outputs = lax.map(one_row, jnp.arange(ROWS, dtype=jnp.int32))
    return jnp.transpose(outputs, (1, 0, 2)).astype(jnp.bfloat16)
```

```python
import functools

import jax
import jax.numpy as jnp
from jax import lax
from jax.experimental import pallas as pl
from jax.experimental.pallas import tpu as pltpu
from jax.sharding import PartitionSpec as P

NX, NZ, NY = 4, 8, 4
HEAD_DIM = 128
SLOTS = 4
CTX = 256
NEG = -1e30
SCALE = HEAD_DIM**-0.5 * 1.4426950408889634
MESH = pl.DeviceIdType.MESH
F32, BF16, I32 = jnp.float32, jnp.bfloat16, jnp.int32


def iota(shape, dim):
    return lax.broadcasted_iota(I32, shape, dim)


def kernel(
    q_hbm, nk_hbm, nv_hbm, k_hbm, v_hbm, len_ref, slot_ref, out_ref,
    q_in, nk_in, nv_in, k_buf, v_buf,
    q_y, kv_y, kv_z, q_all,
    o_x, ml_x, o_x_in, ml_x_in, o_z, ml_z, o_z_in, ml_z_in, fin, fin_in,
    in_sem, cache_sem,
    qy_s, qy_r, kvy_s, kvy_r, kvz_s, kvz_r, qz_s, qz_r, qx_s, qx_r,
    ox_s, ox_r, mx_s, mx_r, oz_s, oz_r, mz_s, mz_r, f_s, f_r,
):
    seq, core = lax.axis_index("seq"), lax.axis_index("rows")
    y = lax.rem(seq, NY)
    z = lax.rem(lax.div(seq, NY), NZ)
    x = lax.div(seq, NY * NZ)

    def at(xx, zz, yy, cc):
        return {"seq": (xx * NZ + zz) * NY + yy, "rows": cc}

    def remote(src, dst, send, recv, target):
        return pltpu.make_async_remote_copy(
            src_ref=src, dst_ref=dst, send_sem=send, recv_sem=recv, device_id=target, device_id_type=MESH
        )

    y_peer = [at(x, z, lax.rem(y + d, NY), core) for d in range(NY)]
    z_peer = [at(x, lax.rem(z + d, NZ), y, core) for d in range(NZ)]
    x_peer = [at(lax.rem(x + d, NX), z, y, core) for d in range(NX)]
    c_peer = [at(x, z, lax.rem(y + d, NY), 1 - core) for d in range(NY)]
    half = lax.div(z, 4)
    zq = lax.rem(z, 4)
    h_peer = [at(x, half * 4 + lax.rem(zq + d, 4), y, core) for d in range(4)]

    loads = [
        pltpu.make_async_copy(q_hbm, q_in, in_sem.at[0]),
        pltpu.make_async_copy(nk_hbm, nk_in, in_sem.at[1]),
        pltpu.make_async_copy(nv_hbm, nv_in, in_sem.at[2]),
    ]
    for c in loads:
        c.start()
    k_loads = [pltpu.make_async_copy(k_hbm.at[s], k_buf.at[s], cache_sem.at[s]) for s in range(SLOTS)]
    v_loads = [pltpu.make_async_copy(v_hbm.at[s], v_buf.at[s], cache_sem.at[SLOTS + s]) for s in range(SLOTS)]
    for c in k_loads + v_loads:
        c.start()

    barrier = pltpu.get_barrier_semaphore()
    peers = y_peer[1:] + z_peer[1:] + x_peer[1:] + c_peer
    for p in peers:
        pl.semaphore_signal(barrier, inc=1, device_id=p, device_id_type=MESH)

    slots = [slot_ref[r] for r in range(8)]
    for c in loads:
        c.wait()

    def by_slot(ref):
        width = ref.shape[2]
        row = iota((8, width), 0)
        wanted = core * SLOTS + lax.rem(row, 4)
        acc = jnp.zeros((8, width), F32)
        for t in range(2):
            whole = ref[t].astype(F32)
            for r in range(8):
                hit = (wanted == slots[r]) & (lax.div(row, 4) == t)
                acc = jnp.where(hit, jnp.broadcast_to(whole[r : r + 1], (8, width)), acc)
        return acc

    mine = by_slot(q_in)
    wide = jnp.concatenate([mine, mine], axis=1)
    wide = jnp.where(lax.div(iota((8, 128), 1), 64) == lax.rem(y, 2), wide, 0.0)
    tile = jnp.concatenate([jnp.where(lax.div(y, 2) == hh, wide, 0.0) for hh in range(2)], axis=0)
    q_y[0] = tile.astype(BF16)

    pl.semaphore_wait(barrier, len(peers))

    qy = [remote(q_y.at[0], q_y.at[d], qy_s.at[d], qy_r.at[d], y_peer[d]) for d in range(1, NY)]
    for c in qy:
        c.start()

    lane = iota((8, 128), 1)
    base = zq * 32 + y * 8
    for i, ref in enumerate((nk_in, nv_in)):
        part = by_slot(ref)
        acc = jnp.zeros((8, 128), F32)
        for f in range(8):
            acc = jnp.where(lane == base + f, jnp.broadcast_to(part[:, f : f + 1], (8, 128)), acc)
        kv_y[0, 8 * i : 8 * i + 8] = acc
    kvy = [remote(kv_y.at[0], kv_y.at[d], kvy_s.at[d], kvy_r.at[d], y_peer[d]) for d in range(1, NY)]
    for c in kvy:
        c.start()

    for c in qy:
        c.wait_recv()
    own_q = (q_y[0] + q_y[1]) + (q_y[2] + q_y[3])
    q_all[x, z] = own_q

    qz = [remote(q_all.at[x, z], q_all.at[x, z], qz_s.at[d], qz_r.at[d], z_peer[d]) for d in range(1, NZ)]
    for c in qz:
        c.start()
    for c in kvy:
        c.wait_recv()
    kv_z[0] = (kv_y[0] + kv_y[1]) + (kv_y[2] + kv_y[3])
    kvz = [remote(kv_z.at[0], kv_z.at[d], kvz_s.at[d], kvz_r.at[d], h_peer[d]) for d in range(1, 4)]
    for c in kvz:
        c.start()

    def z_in(d):
        zz = lax.rem(z + NZ - d, NZ)
        return remote(q_all.at[x, zz], q_all.at[x, zz], qz_s.at[d], qz_r.at[d], z_peer[d])

    for d in range(1, NZ):
        z_in(d).wait_recv()

    qx = [remote(q_all.at[x], q_all.at[x], qx_s.at[d], qx_r.at[d], x_peer[d]) for d in range(1, NX)]
    for c in qx:
        c.start()

    def x_in(d):
        xx = lax.rem(x + NX - d, NX)
        return remote(q_all.at[xx], q_all.at[xx], qx_s.at[d], qx_r.at[d], x_peer[d])

    slot_of = lax.rem(iota((64, CTX), 0), SLOTS)
    limit = jnp.zeros((64, CTX), I32)
    for s in range(SLOTS):
        n = jnp.int32(0)
        for r in range(8):
            n = n + jnp.where(slots[r] == core * SLOTS + s, len_ref[r], 0)
        limit = jnp.where(slot_of == s, n, limit)
    valid = seq * CTX + iota((64, CTX), 1) < limit
    slot_out = lax.rem(iota((64, HEAD_DIM), 0), SLOTS)
    lane16 = iota((16, 128), 1)

    for c in k_loads + v_loads:
        c.wait()

    def attend(xb, slot):
        ml = jnp.zeros((16, 128), F32)
        for j in range(2):
            cols = pl.ds(pl.multiple_of((xb * 2 + j) * HEAD_DIM, HEAD_DIM), HEAD_DIM)
            q = q_all[xb, 4 * j : 4 * j + 4].reshape(64, HEAD_DIM)
            scores = None
            for s in range(SLOTS):
                part = lax.dot_general(q, k_buf[s, :, cols], (((1,), (1,)), ((), ())), preferred_element_type=F32)
                scores = part if s == 0 else jnp.where(slot_of == s, part, scores)
            scores = jnp.where(valid, scores * SCALE, NEG)
            top = jnp.max(scores, axis=1, keepdims=True)
            p = jnp.where(valid, jnp.exp2(scores - top), 0.0)
            total = jnp.sum(p, axis=1, keepdims=True)
            p = p.astype(BF16)
            out = None
            for s in range(SLOTS):
                part = jnp.dot(p, v_buf[s, :, cols], preferred_element_type=F32)
                out = part if s == 0 else jnp.where(slot_out == s, part, out)
            o_x[slot, 4 * j : 4 * j + 4] = out.astype(BF16).reshape(4, 16, HEAD_DIM)
            for zz in range(4):
                rows = slice(16 * zz, 16 * zz + 16)
                ml = jnp.where(lane16 == 4 * j + zz, top[rows], ml)
                ml = jnp.where(lane16 == 64 + 4 * j + zz, total[rows], ml)
        ml_x[slot] = ml

    back = []
    for d in range(1, NX):
        x_in(d).wait_recv()
        attend(lax.rem(x + NX - d, NX), d)
        target = x_peer[NX - d]
        back.append(remote(o_x.at[d], o_x_in.at[d], ox_s.at[d], ox_r.at[d], target))
        back.append(remote(ml_x.at[d], ml_x_in.at[d], mx_s.at[d], mx_r.at[d], target))
        back[-2].start()
        back[-1].start()
    attend(x, 0)

    for c in kvz:
        c.wait_recv()
    kv = (kv_z[0] + kv_z[1]) + (kv_z[2] + kv_z[3])
    row8 = iota((8, 128), 0)

    def spread(block):
        turned = jnp.concatenate([block[4:8], block[0:4]], axis=0)
        return jnp.where(row8 < 4, block, turned), jnp.where(row8 < 4, turned, block)

    key0, key1 = spread(kv[0:8])
    val0, val1 = spread(kv[8:16])
    both = lambda a: jnp.concatenate([a, a], axis=0)
    qf = own_q.astype(F32)
    second = lax.rem(lax.div(iota((16, 1), 0), 4), 2) == 1
    here = y == 0
    s0 = jnp.sum(qf * both(key0), axis=1, keepdims=True) * SCALE
    s1 = jnp.where(second, jnp.sum(qf * both(key1), axis=1, keepdims=True) * SCALE, NEG)
    new_top = jnp.maximum(s0, s1)
    p0 = jnp.exp2(s0 - new_top)
    p1 = jnp.where(second, jnp.exp2(s1 - new_top), 0.0)
    new_out = p0 * both(val0) + p1 * both(val1)
    new_top = jnp.where(here, new_top, NEG)
    new_total = jnp.where(here, p0 + p1, 0.0)
    new_out = jnp.where(here, new_out, 0.0)

    for c in back:
        c.wait_recv()
    mls = [ml_x[0]] + [ml_x_in[d] for d in range(1, NX)]

    def weigh(mls):
        top = functools.reduce(jnp.maximum, mls)
        factors = [jnp.exp2(m - top) for m in mls]
        total = sum(pltpu.roll(f, 64, 1) * m for f, m in zip(factors, mls))
        return factors, jnp.where(lane16 < 64, top, total)

    factors, ml = weigh(mls)
    ml_z[...] = ml
    for zz in range(NZ):
        acc = factors[0][:, zz : zz + 1] * o_x[0, zz].astype(F32)
        for d in range(1, NX):
            acc = acc + factors[d][:, zz : zz + 1] * o_x_in[d, zz].astype(F32)
        o_z[zz] = acc.astype(BF16)

    oz, mz = [], []
    for d in range(1, NZ):
        zz = lax.rem(z + d, NZ)
        oz.append(remote(o_z.at[zz], o_z_in.at[d], oz_s.at[d], oz_r.at[d], z_peer[d]))
        mz.append(remote(ml_z, ml_z_in.at[d], mz_s.at[d], mz_r.at[d], z_peer[d]))
        oz[-1].start()
        mz[-1].start()
    for c in oz + mz:
        c.wait_recv()
    mls = [ml] + [ml_z_in[d] for d in range(1, NZ)]
    outs = [o_z[z]] + [o_z_in[d] for d in range(1, NZ)]

    def column(tile, at_lane):
        return jnp.sum(jnp.where(lane16 == at_lane, tile, 0.0), axis=1, keepdims=True)

    factors, ml = weigh(mls)
    top, total = column(ml, z), column(ml, z + 64)
    acc = sum(column(f, z) * o.astype(F32) for f, o in zip(factors, outs))
    best = jnp.maximum(top, new_top)
    old_factor, new_factor = jnp.exp2(top - best), jnp.exp2(new_top - best)
    acc = old_factor * acc + new_factor * new_out
    total = old_factor * total + new_factor * new_total

    for yy in range(NY):
        rows = slice(8 * (yy // 2), 8 * (yy // 2) + 8)
        part = acc[rows]
        if yy % 2:
            part = pltpu.roll(part, 64, 1)
        fin[yy] = jnp.where(lane < 64, part, jnp.where(lane < 96, best[rows], total[rows]))
    f = []
    for d in range(NY):
        for other in range(2):
            if d or other:
                yy = lax.rem(y + d, NY)
                i = other * NY + d
                f.append(remote(fin.at[yy], fin_in.at[i], f_s.at[i], f_r.at[i], (c_peer if other else y_peer)[d]))
    for c in f:
        c.start()
    for c in f:
        c.wait_recv()

    parts = []
    for other in range(2):
        tiles = [fin[y] if i == 0 else fin_in[i] for i in range(other * NY, other * NY + NY)]
        top = functools.reduce(jnp.maximum, tiles)
        acc = sum(jnp.exp2(t - top)[:, 64:65] * t for t in tiles)
        parts.append(acc[:, :64] / acc[:, 96:97])
    row = iota((8, 64), 0)
    slot_row = jnp.zeros((8, 64), I32)
    for r in range(8):
        slot_row = jnp.where(row == r, slots[r], slot_row)
    for t in range(2):
        result = jnp.zeros((8, 64), F32)
        for other in range(2):
            group = core + other - 2 * core * other
            for s in range(SLOTS):
                i = t * 4 + s
                found = slot_row == group * SLOTS + s
                result = jnp.where(found, jnp.broadcast_to(parts[other][i : i + 1], (8, 64)), result)
        out_ref[t] = result.astype(BF16)

    for c in qy + kvy + qz + kvz + qx + back + oz + mz + f:
        c.wait_send()


def local(queries, new_keys, new_values, key_cache, value_cache, lengths, row_slot):
    anywhere = pl.BlockSpec(memory_space=pl.ANY)
    scalars = pl.BlockSpec(memory_space=pltpu.SMEM)
    sem = pltpu.SemaphoreType.DMA
    return pl.pallas_call(
        kernel,
        out_shape=jax.ShapeDtypeStruct(queries.shape, BF16),
        in_specs=[anywhere] * 5 + [scalars] * 2,
        out_specs=pl.BlockSpec(memory_space=pltpu.VMEM),
        scratch_shapes=[
            pltpu.VMEM(queries.shape, BF16),
            pltpu.VMEM(new_keys.shape, BF16),
            pltpu.VMEM(new_values.shape, BF16),
            pltpu.VMEM(key_cache.shape, BF16),
            pltpu.VMEM(value_cache.shape, BF16),
            pltpu.VMEM((NY, 16, 128), BF16),
            pltpu.VMEM((NY, 16, 128), F32),
            pltpu.VMEM((4, 16, 128), F32),
            pltpu.VMEM((NX, NZ, 16, 128), BF16),
            pltpu.VMEM((NX, NZ, 16, 128), BF16),
            pltpu.VMEM((NX, 16, 128), F32),
            pltpu.VMEM((NX, NZ, 16, 128), BF16),
            pltpu.VMEM((NX, 16, 128), F32),
            pltpu.VMEM((NZ, 16, 128), BF16),
            pltpu.VMEM((16, 128), F32),
            pltpu.VMEM((NZ, 16, 128), BF16),
            pltpu.VMEM((NZ, 16, 128), F32),
            pltpu.VMEM((NY, 8, 128), F32),
            pltpu.VMEM((2 * NY, 8, 128), F32),
            sem((3,)), sem((2 * SLOTS,)),
            sem((NY,)), sem((NY,)), sem((NY,)), sem((NY,)), sem((4,)), sem((4,)),
            sem((NZ,)), sem((NZ,)), sem((NX,)), sem((NX,)),
            sem((NX,)), sem((NX,)), sem((NX,)), sem((NX,)),
            sem((NZ,)), sem((NZ,)), sem((NZ,)), sem((NZ,)),
            sem((2 * NY,)), sem((2 * NY,)),
        ],
        compiler_params=pltpu.CompilerParams(
            collective_id=0, has_side_effects=True, vmem_limit_bytes=48 * 1024 * 1024
        ),
    )(queries, new_keys, new_values, key_cache, value_cache, lengths, row_slot)


def solution(mesh):
    in_specs = (
        P(None, None, "seq"),
        P(None, None, "seq"),
        P(None, None, "seq"),
        P("rows", "seq", None),
        P("rows", "seq", None),
        P(),
        P(),
    )
    out_specs = P(None, None, "seq")
    return jax.shard_map(local, mesh=mesh, in_specs=in_specs, out_specs=out_specs, check_vma=False)
```

```python
import functools

import jax
import jax.numpy as jnp
from jax import lax
from jax.experimental import pallas as pl
from jax.experimental.pallas import tpu as pltpu
from jax.sharding import PartitionSpec as P

NX, NZ, NY = 4, 8, 4
HEAD_DIM = 128
SLOTS = 4
CTX = 256
NEG = -1e30
SCALE = HEAD_DIM**-0.5 * 1.4426950408889634
MESH = pl.DeviceIdType.MESH
F32, BF16, I32 = jnp.float32, jnp.bfloat16, jnp.int32


def iota(shape, dim):
    return lax.broadcasted_iota(I32, shape, dim)


def kernel(
    q_hbm, nk_hbm, nv_hbm, k_hbm, v_hbm, len_hbm, slot_hbm, out_ref,
    q_in, nk_in, nv_in, len_ref, slot_ref, k_buf, v_buf,
    q_y, kv_y, kv_z, q_all,
    o_x, ml_x, o_x_in, ml_x_in, o_z, ml_z, o_z_in, ml_z_in, fin, fin_in,
    in_sem, cache_sem,
    qy_s, qy_r, kvy_s, kvy_r, kvz_s, kvz_r, qz_s, qz_r, qx_s, qx_r,
    ox_s, ox_r, mx_s, mx_r, oz_s, oz_r, mz_s, mz_r, f_s, f_r,
):
    seq, core = lax.axis_index("seq"), lax.axis_index("rows")
    y = lax.rem(seq, NY)
    z = lax.rem(lax.div(seq, NY), NZ)
    x = lax.div(seq, NY * NZ)

    def at(xx, zz, yy, cc):
        return {"seq": (xx * NZ + zz) * NY + yy, "rows": cc}

    def remote(src, dst, send, recv, target):
        return pltpu.make_async_remote_copy(
            src_ref=src, dst_ref=dst, send_sem=send, recv_sem=recv, device_id=target, device_id_type=MESH
        )

    y_peer = [at(x, z, lax.rem(y + d, NY), core) for d in range(NY)]
    z_peer = [at(x, lax.rem(z + d, NZ), y, core) for d in range(NZ)]
    x_peer = [at(lax.rem(x + d, NX), z, y, core) for d in range(NX)]
    c_peer = [at(x, z, lax.rem(y + d, NY), 1 - core) for d in range(NY)]
    half = lax.div(z, 4)
    zq = lax.rem(z, 4)
    h_peer = [at(x, half * 4 + lax.rem(zq + d, 4), y, core) for d in range(4)]

    loads = [
        pltpu.make_async_copy(q_hbm, q_in, in_sem.at[0]),
        pltpu.make_async_copy(nk_hbm, nk_in, in_sem.at[1]),
        pltpu.make_async_copy(nv_hbm, nv_in, in_sem.at[2]),
        pltpu.make_async_copy(slot_hbm, slot_ref, in_sem.at[3]),
        pltpu.make_async_copy(len_hbm, len_ref, in_sem.at[4]),
    ]
    for c in loads:
        c.start()
    k_loads = [pltpu.make_async_copy(k_hbm.at[s], k_buf.at[s], cache_sem.at[s]) for s in range(SLOTS)]
    v_loads = [pltpu.make_async_copy(v_hbm.at[s], v_buf.at[s], cache_sem.at[SLOTS + s]) for s in range(SLOTS)]
    for c in k_loads + v_loads:
        c.start()

    barrier = pltpu.get_barrier_semaphore()
    peers = y_peer[1:] + z_peer[1:] + x_peer[1:] + c_peer
    for p in peers:
        pl.semaphore_signal(barrier, inc=1, device_id=p, device_id_type=MESH)

    for c in loads:
        c.wait()
    slots = [slot_ref[r] for r in range(8)]

    def by_slot(ref):
        width = ref.shape[2]
        row = iota((8, width), 0)
        wanted = core * SLOTS + lax.rem(row, 4)
        acc = jnp.zeros((8, width), F32)
        for t in range(2):
            whole = ref[t].astype(F32)
            for r in range(8):
                hit = (wanted == slots[r]) & (lax.div(row, 4) == t)
                acc = jnp.where(hit, jnp.broadcast_to(whole[r : r + 1], (8, width)), acc)
        return acc

    mine = by_slot(q_in)
    wide = jnp.concatenate([mine, mine], axis=1)
    wide = jnp.where(lax.div(iota((8, 128), 1), 64) == lax.rem(y, 2), wide, 0.0)
    tile = jnp.concatenate([jnp.where(lax.div(y, 2) == hh, wide, 0.0) for hh in range(2)], axis=0)
    q_y[0] = tile.astype(BF16)

    pl.semaphore_wait(barrier, len(peers))

    qy = [remote(q_y.at[0], q_y.at[d], qy_s.at[d], qy_r.at[d], y_peer[d]) for d in range(1, NY)]
    for c in qy:
        c.start()

    lane = iota((8, 128), 1)
    base = zq * 32 + y * 8
    for i, ref in enumerate((nk_in, nv_in)):
        part = by_slot(ref)
        acc = jnp.zeros((8, 128), F32)
        for f in range(8):
            acc = jnp.where(lane == base + f, jnp.broadcast_to(part[:, f : f + 1], (8, 128)), acc)
        kv_y[0, 8 * i : 8 * i + 8] = acc
    kvy = [remote(kv_y.at[0], kv_y.at[d], kvy_s.at[d], kvy_r.at[d], y_peer[d]) for d in range(1, NY)]
    for c in kvy:
        c.start()

    for c in qy:
        c.wait_recv()
    own_q = (q_y[0] + q_y[1]) + (q_y[2] + q_y[3])
    q_all[x, z] = own_q

    qz = [remote(q_all.at[x, z], q_all.at[x, z], qz_s.at[d], qz_r.at[d], z_peer[d]) for d in range(1, NZ)]
    for c in qz:
        c.start()
    for c in kvy:
        c.wait_recv()
    kv_z[0] = (kv_y[0] + kv_y[1]) + (kv_y[2] + kv_y[3])
    kvz = [remote(kv_z.at[0], kv_z.at[d], kvz_s.at[d], kvz_r.at[d], h_peer[d]) for d in range(1, 4)]
    for c in kvz:
        c.start()

    def z_in(d):
        zz = lax.rem(z + NZ - d, NZ)
        return remote(q_all.at[x, zz], q_all.at[x, zz], qz_s.at[d], qz_r.at[d], z_peer[d])

    for d in range(1, NZ):
        z_in(d).wait_recv()

    qx = [remote(q_all.at[x], q_all.at[x], qx_s.at[d], qx_r.at[d], x_peer[d]) for d in range(1, NX)]
    for c in qx:
        c.start()

    def x_in(d):
        xx = lax.rem(x + NX - d, NX)
        return remote(q_all.at[xx], q_all.at[xx], qx_s.at[d], qx_r.at[d], x_peer[d])

    slot_of = lax.rem(iota((64, CTX), 0), SLOTS)
    limit = jnp.zeros((64, CTX), I32)
    for s in range(SLOTS):
        n = jnp.int32(0)
        for r in range(8):
            n = n + jnp.where(slots[r] == core * SLOTS + s, len_ref[r], 0)
        limit = jnp.where(slot_of == s, n, limit)
    valid = seq * CTX + iota((64, CTX), 1) < limit
    slot_out = lax.rem(iota((64, HEAD_DIM), 0), SLOTS)
    lane16 = iota((16, 128), 1)

    for c in k_loads + v_loads:
        c.wait()

    def attend(xb, slot):
        ml = jnp.zeros((16, 128), F32)
        for j in range(2):
            cols = pl.ds(pl.multiple_of((xb * 2 + j) * HEAD_DIM, HEAD_DIM), HEAD_DIM)
            q = q_all[xb, 4 * j : 4 * j + 4].reshape(64, HEAD_DIM)
            scores = None
            for s in range(SLOTS):
                part = lax.dot_general(q, k_buf[s, :, cols], (((1,), (1,)), ((), ())), preferred_element_type=F32)
                scores = part if s == 0 else jnp.where(slot_of == s, part, scores)
            scores = jnp.where(valid, scores * SCALE, NEG)
            top = jnp.max(scores, axis=1, keepdims=True)
            p = jnp.where(valid, jnp.exp2(scores - top), 0.0)
            total = jnp.sum(p, axis=1, keepdims=True)
            p = p.astype(BF16)
            out = None
            for s in range(SLOTS):
                part = jnp.dot(p, v_buf[s, :, cols], preferred_element_type=F32)
                out = part if s == 0 else jnp.where(slot_out == s, part, out)
            o_x[slot, 4 * j : 4 * j + 4] = out.astype(BF16).reshape(4, 16, HEAD_DIM)
            for zz in range(4):
                rows = slice(16 * zz, 16 * zz + 16)
                ml = jnp.where(lane16 == 4 * j + zz, top[rows], ml)
                ml = jnp.where(lane16 == 64 + 4 * j + zz, total[rows], ml)
        ml_x[slot] = ml

    back = []
    for d in range(1, NX):
        x_in(d).wait_recv()
        attend(lax.rem(x + NX - d, NX), d)
        target = x_peer[NX - d]
        back.append(remote(o_x.at[d], o_x_in.at[d], ox_s.at[d], ox_r.at[d], target))
        back.append(remote(ml_x.at[d], ml_x_in.at[d], mx_s.at[d], mx_r.at[d], target))
        back[-2].start()
        back[-1].start()
    attend(x, 0)

    for c in kvz:
        c.wait_recv()
    kv = (kv_z[0] + kv_z[1]) + (kv_z[2] + kv_z[3])
    row8 = iota((8, 128), 0)

    def spread(block):
        turned = jnp.concatenate([block[4:8], block[0:4]], axis=0)
        return jnp.where(row8 < 4, block, turned), jnp.where(row8 < 4, turned, block)

    key0, key1 = spread(kv[0:8])
    val0, val1 = spread(kv[8:16])
    both = lambda a: jnp.concatenate([a, a], axis=0)
    qf = own_q.astype(F32)
    second = lax.rem(lax.div(iota((16, 1), 0), 4), 2) == 1
    here = y == 0
    s0 = jnp.sum(qf * both(key0), axis=1, keepdims=True) * SCALE
    s1 = jnp.where(second, jnp.sum(qf * both(key1), axis=1, keepdims=True) * SCALE, NEG)
    new_top = jnp.maximum(s0, s1)
    p0 = jnp.exp2(s0 - new_top)
    p1 = jnp.where(second, jnp.exp2(s1 - new_top), 0.0)
    new_out = p0 * both(val0) + p1 * both(val1)
    new_top = jnp.where(here, new_top, NEG)
    new_total = jnp.where(here, p0 + p1, 0.0)
    new_out = jnp.where(here, new_out, 0.0)

    for c in back:
        c.wait_recv()
    mls = [ml_x[0]] + [ml_x_in[d] for d in range(1, NX)]

    def weigh(mls):
        top = functools.reduce(jnp.maximum, mls)
        factors = [jnp.exp2(m - top) for m in mls]
        total = sum(pltpu.roll(f, 64, 1) * m for f, m in zip(factors, mls))
        return factors, jnp.where(lane16 < 64, top, total)

    factors, ml = weigh(mls)
    ml_z[...] = ml
    for zz in range(NZ):
        acc = factors[0][:, zz : zz + 1] * o_x[0, zz].astype(F32)
        for d in range(1, NX):
            acc = acc + factors[d][:, zz : zz + 1] * o_x_in[d, zz].astype(F32)
        o_z[zz] = acc.astype(BF16)

    oz, mz = [], []
    for d in range(1, NZ):
        zz = lax.rem(z + d, NZ)
        oz.append(remote(o_z.at[zz], o_z_in.at[d], oz_s.at[d], oz_r.at[d], z_peer[d]))
        mz.append(remote(ml_z, ml_z_in.at[d], mz_s.at[d], mz_r.at[d], z_peer[d]))
        oz[-1].start()
        mz[-1].start()
    for c in oz + mz:
        c.wait_recv()
    mls = [ml] + [ml_z_in[d] for d in range(1, NZ)]
    outs = [o_z[z]] + [o_z_in[d] for d in range(1, NZ)]

    def column(tile, at_lane):
        return jnp.sum(jnp.where(lane16 == at_lane, tile, 0.0), axis=1, keepdims=True)

    factors, ml = weigh(mls)
    top, total = column(ml, z), column(ml, z + 64)
    acc = sum(column(f, z) * o.astype(F32) for f, o in zip(factors, outs))
    best = jnp.maximum(top, new_top)
    old_factor, new_factor = jnp.exp2(top - best), jnp.exp2(new_top - best)
    acc = old_factor * acc + new_factor * new_out
    total = old_factor * total + new_factor * new_total

    for yy in range(NY):
        rows = slice(8 * (yy // 2), 8 * (yy // 2) + 8)
        part = acc[rows]
        if yy % 2:
            part = pltpu.roll(part, 64, 1)
        fin[yy] = jnp.where(lane < 64, part, jnp.where(lane < 96, best[rows], total[rows]))
    f = []
    for d in range(NY):
        for other in range(2):
            if d or other:
                yy = lax.rem(y + d, NY)
                i = other * NY + d
                f.append(remote(fin.at[yy], fin_in.at[i], f_s.at[i], f_r.at[i], (c_peer if other else y_peer)[d]))
    for c in f:
        c.start()
    for c in f:
        c.wait_recv()

    parts = []
    for other in range(2):
        tiles = [fin[y] if i == 0 else fin_in[i] for i in range(other * NY, other * NY + NY)]
        top = functools.reduce(jnp.maximum, tiles)
        acc = sum(jnp.exp2(t - top)[:, 64:65] * t for t in tiles)
        parts.append(acc[:, :64] / acc[:, 96:97])
    row = iota((8, 64), 0)
    slot_row = jnp.zeros((8, 64), I32)
    for r in range(8):
        slot_row = jnp.where(row == r, slots[r], slot_row)
    for t in range(2):
        result = jnp.zeros((8, 64), F32)
        for other in range(2):
            group = core + other - 2 * core * other
            for s in range(SLOTS):
                i = t * 4 + s
                found = slot_row == group * SLOTS + s
                result = jnp.where(found, jnp.broadcast_to(parts[other][i : i + 1], (8, 64)), result)
        out_ref[t] = result.astype(BF16)

    for c in qy + kvy + qz + kvz + qx + back + oz + mz + f:
        c.wait_send()


def local(queries, new_keys, new_values, key_cache, value_cache, lengths, row_slot):
    sem = pltpu.SemaphoreType.DMA
    return pl.pallas_call(
        kernel,
        out_shape=jax.ShapeDtypeStruct(queries.shape, BF16),
        in_specs=[pl.BlockSpec(memory_space=pltpu.HBM)] * 7,
        out_specs=pl.BlockSpec(memory_space=pltpu.VMEM),
        scratch_shapes=[
            pltpu.VMEM(queries.shape, BF16),
            pltpu.VMEM(new_keys.shape, BF16),
            pltpu.VMEM(new_values.shape, BF16),
            pltpu.SMEM(lengths.shape, I32),
            pltpu.SMEM(row_slot.shape, I32),
            pltpu.VMEM(key_cache.shape, BF16),
            pltpu.VMEM(value_cache.shape, BF16),
            pltpu.VMEM((NY, 16, 128), BF16),
            pltpu.VMEM((NY, 16, 128), F32),
            pltpu.VMEM((4, 16, 128), F32),
            pltpu.VMEM((NX, NZ, 16, 128), BF16),
            pltpu.VMEM((NX, NZ, 16, 128), BF16),
            pltpu.VMEM((NX, 16, 128), F32),
            pltpu.VMEM((NX, NZ, 16, 128), BF16),
            pltpu.VMEM((NX, 16, 128), F32),
            pltpu.VMEM((NZ, 16, 128), BF16),
            pltpu.VMEM((16, 128), F32),
            pltpu.VMEM((NZ, 16, 128), BF16),
            pltpu.VMEM((NZ, 16, 128), F32),
            pltpu.VMEM((NY, 8, 128), F32),
            pltpu.VMEM((2 * NY, 8, 128), F32),
            sem((5,)), sem((2 * SLOTS,)),
            sem((NY,)), sem((NY,)), sem((NY,)), sem((NY,)), sem((4,)), sem((4,)),
            sem((NZ,)), sem((NZ,)), sem((NX,)), sem((NX,)),
            sem((NX,)), sem((NX,)), sem((NX,)), sem((NX,)),
            sem((NZ,)), sem((NZ,)), sem((NZ,)), sem((NZ,)),
            sem((2 * NY,)), sem((2 * NY,)),
        ],
        compiler_params=pltpu.CompilerParams(
            collective_id=0, has_side_effects=True, vmem_limit_bytes=64 * 1024 * 1024
        ),
    )(queries, new_keys, new_values, key_cache, value_cache, lengths, row_slot)


def solution(mesh):
    in_specs = (
        P(None, None, "seq"),
        P(None, None, "seq"),
        P(None, None, "seq"),
        P("rows", "seq", None),
        P("rows", "seq", None),
        P(),
        P(),
    )
    out_specs = P(None, None, "seq")
    return jax.shard_map(local, mesh=mesh, in_specs=in_specs, out_specs=out_specs, check_vma=False)
```

```python
import functools

import jax
import jax.numpy as jnp
from jax import lax
from jax.experimental import pallas as pl
from jax.experimental.pallas import tpu as pltpu
from jax.sharding import PartitionSpec as P

NX, NZ, NY = 4, 8, 4
HEAD_DIM = 128
SLOTS = 4
CTX = 256
NEG = -1e30
SCALE = HEAD_DIM**-0.5 * 1.4426950408889634
MESH = pl.DeviceIdType.MESH
F32, BF16, I32 = jnp.float32, jnp.bfloat16, jnp.int32


def iota(shape, dim):
    return lax.broadcasted_iota(I32, shape, dim)


def kernel(
    q_hbm, nk_hbm, nv_hbm, k_hbm, v_hbm, len_hbm, slot_hbm, out_ref,
    q_in, nk_in, nv_in, len_ref, slot_ref, k_buf, v_buf,
    new_y, new_z, q_z, q_xy, o_xy, ml_xy, o_in, ml_in, fin, fin_in,
    in_sem, cache_sem,
    ny_s, ny_r, nz_s, nz_r, qz_s, qz_r, qxy_s, qxy_r, o_s, o_r, ml_s, ml_r, f_s, f_r,
):
    seq, core = lax.axis_index("seq"), lax.axis_index("rows")
    y = lax.rem(seq, NY)
    z = lax.rem(lax.div(seq, NY), NZ)
    x = lax.div(seq, NY * NZ)
    pair, half = lax.div(y, 2), lax.rem(y, 2)
    zq = lax.rem(z, 4)

    def at(xx, zz, yy, cc):
        return {"seq": (xx * NZ + zz) * NY + yy, "rows": cc}

    def remote(src, dst, send, recv, target):
        return pltpu.make_async_remote_copy(
            src_ref=src, dst_ref=dst, send_sem=send, recv_sem=recv, device_id=target, device_id_type=MESH
        )

    z_peer = [[at(x, lax.rem(z + d, NZ), y, c) for d in range(NZ)] for c in (core, 1 - core)]
    xy_peer = [[at(lax.rem(x + a, NX), z, lax.rem(y + b, NY), core) for b in range(NY)] for a in range(NX)]
    half_peer = [at(x, z - zq + lax.rem(zq + d, 4), y, core) for d in range(4)]
    others = [(a, b) for a in range(NX) for b in range(NY) if a or b]

    loads = [
        pltpu.make_async_copy(q_hbm, q_in, in_sem.at[0]),
        pltpu.make_async_copy(slot_hbm, slot_ref, in_sem.at[1]),
        pltpu.make_async_copy(nk_hbm, nk_in, in_sem.at[2]),
        pltpu.make_async_copy(nv_hbm, nv_in, in_sem.at[3]),
        pltpu.make_async_copy(len_hbm, len_ref, in_sem.at[4]),
    ]
    for c in loads:
        c.start()

    barrier = pltpu.get_barrier_semaphore()
    peers = z_peer[0][1:] + z_peer[1] + [xy_peer[a][b] for a, b in others]
    for p in peers:
        pl.semaphore_signal(barrier, inc=1, device_id=p, device_id_type=MESH)

    k_loads = [pltpu.make_async_copy(k_hbm.at[s], k_buf.at[s], cache_sem.at[s]) for s in range(SLOTS)]
    v_loads = [pltpu.make_async_copy(v_hbm.at[s], v_buf.at[s], cache_sem.at[SLOTS + s]) for s in range(SLOTS)]
    for c in k_loads + v_loads:
        c.start()
    for c in loads:
        c.wait()
    slots = [slot_ref[r] for r in range(8)]

    def by_slot(ref):
        width = ref.shape[2]
        row = iota((8, width), 0)
        wanted = core * SLOTS + lax.rem(row, 4)
        acc = jnp.zeros((8, width), F32)
        for t in range(2):
            whole = ref[t].astype(F32)
            for r in range(8):
                hit = (wanted == slots[r]) & (lax.div(row, 4) == t)
                acc = jnp.where(hit, jnp.broadcast_to(whole[r : r + 1], (8, width)), acc)
        return acc

    lane, row8 = iota((8, 128), 1), iota((8, 128), 0)
    mine = by_slot(q_in)
    q_z[z] = jnp.concatenate([mine[0:4], mine[4:8]], axis=1)

    pl.semaphore_wait(barrier, len(peers))

    def qz_copy(d, origin):
        return remote(q_z.at[origin], q_z.at[origin], qz_s.at[d], qz_r.at[d], z_peer[0][d])

    qz = [qz_copy(d, z) for d in (4, 3, 5, 2, 6, 1, 7)]
    for c in qz:
        c.start()

    base = zq * 32 + y * 8
    for i, ref in enumerate((nk_in, nv_in)):
        part = by_slot(ref)
        acc = jnp.zeros((8, 128), F32)
        for f in range(8):
            acc = jnp.where(lane == base + f, jnp.broadcast_to(part[:, f : f + 1], (8, 128)), acc)
        new_y[0, 8 * i : 8 * i + 8] = acc
    new_y[0, 16:24] = jnp.where(lax.div(lane, 64) == half, jnp.concatenate([mine, mine], axis=1), 0.0)
    ny = [remote(new_y.at[0], new_y.at[d], ny_s.at[d], ny_r.at[d], xy_peer[0][d]) for d in range(1, NY)]
    for c in ny:
        c.start()

    slot_of = lax.rem(iota((64, CTX), 0), SLOTS)
    limit = jnp.zeros((64, CTX), I32)
    for s in range(SLOTS):
        n = jnp.int32(0)
        for r in range(8):
            n = n + jnp.where(slots[r] == core * SLOTS + s, len_ref[r], 0)
        limit = jnp.where(slot_of == s, n, limit)
    valid = seq * CTX + iota((64, CTX), 1) < limit
    slot_out = lax.rem(iota((64, HEAD_DIM), 0), SLOTS)
    left16, left32 = iota((16, 128), 1) < 64, iota((32, 128), 1) < 64

    for d in range(1, NZ):
        qz_copy(d, lax.rem(z + NZ - d, NZ)).wait_recv()
    q_xy[x, y] = jnp.concatenate([q_z[i] for i in range(NZ)], axis=0).astype(BF16)

    def qxy_copy(a, b, xx, yy):
        return remote(q_xy.at[xx, yy], q_xy.at[xx, yy], qxy_s.at[a, b], qxy_r.at[a, b], xy_peer[a][b])

    qxy = [qxy_copy(a, b, x, y) for a in (2, 1, 3, 0) for b in (2, 1, 3, 0) if a or b]
    for c in qxy:
        c.start()

    for c in ny:
        c.wait_recv()
    new_z[0] = (new_y[0, 0:16] + new_y[1, 0:16]) + (new_y[2, 0:16] + new_y[3, 0:16])
    nz = [remote(new_z.at[0], new_z.at[d], nz_s.at[d], nz_r.at[d], half_peer[d]) for d in range(1, 4)]
    for c in nz:
        c.start()

    for c in k_loads + v_loads:
        c.wait()

    def attend(xb, slot):
        turned = []
        for hh in range(2):
            a, b = q_xy[xb, 2 * hh].astype(F32), q_xy[xb, 2 * hh + 1].astype(F32)
            turned.append(jnp.where(left32, a, pltpu.roll(b, 64, 1)).astype(BF16))
            turned.append(jnp.where(left32, pltpu.roll(a, 64, 1), b).astype(BF16))
        ml = jnp.zeros((8, 128), F32)
        for j in range(2):
            cols = pl.ds(pl.multiple_of((xb * 2 + j) * HEAD_DIM, HEAD_DIM), HEAD_DIM)
            q = jnp.concatenate([u[16 * j : 16 * j + 16] for u in turned], axis=0)
            scores = None
            for s in range(SLOTS):
                part = lax.dot_general(q, k_buf[s, :, cols], (((1,), (1,)), ((), ())), preferred_element_type=F32)
                scores = part if s == 0 else jnp.where(slot_of == s, part, scores)
            scores = jnp.where(valid, scores * SCALE, NEG)
            top = jnp.max(scores, axis=1, keepdims=True)
            p = jnp.where(valid, jnp.exp2(scores - top), 0.0)
            total = jnp.sum(p, axis=1, keepdims=True)
            p = p.astype(BF16)
            out = None
            for s in range(SLOTS):
                part = jnp.dot(p, v_buf[s, :, cols], preferred_element_type=F32)
                out = part if s == 0 else jnp.where(slot_out == s, part, out)
            for hh in range(2):
                first, second = out[32 * hh : 32 * hh + 16], out[32 * hh + 16 : 32 * hh + 32]
                rows = slice(16 * j, 16 * j + 16)
                o_xy[slot, 2 * hh, rows] = jnp.where(left16, first, pltpu.roll(second, 64, 1)).astype(BF16)
                o_xy[slot, 2 * hh + 1, rows] = jnp.where(left16, pltpu.roll(first, 64, 1), second).astype(BF16)
                for t in range(2):
                    for rh in range(2):
                        here = slice(32 * hh + 16 * t + 8 * rh, 32 * hh + 16 * t + 8 * rh + 8)
                        i = hh * 8 + j * 4 + t * 2 + rh
                        ml = jnp.where(lane == i, top[here], ml)
                        ml = jnp.where(lane == 64 + i, total[here], ml)
        ml_xy[slot] = ml

    back = {}
    for a in range(NX):
        xb = lax.rem(x + NX - a, NX)
        for b in range(NY):
            if a or b:
                qxy_copy(a, b, xb, lax.rem(y + NY - b, NY)).wait_recv()
        attend(xb, a)
        for b in (2, 1, 3, 0):
            if a or b:
                target = xy_peer[(NX - a) % NX][b]
                yy = lax.rem(y + b, NY)
                back[a, b] = (
                    remote(o_xy.at[a, yy], o_in.at[a, b], o_s.at[a, b], o_r.at[a, b], target),
                    remote(ml_xy.at[a], ml_in.at[a, b], ml_s.at[a, b], ml_r.at[a, b], target),
                )
                for c in back[a, b]:
                    c.start()

    for c in nz:
        c.wait_recv()
    new = (new_z[0] + new_z[1]) + (new_z[2] + new_z[3])

    def spread(block):
        turned = jnp.concatenate([block[4:8], block[0:4]], axis=0)
        return jnp.where(row8 < 4, block, turned), jnp.where(row8 < 4, turned, block)

    key0, key1 = spread(new[0:8])
    val0, val1 = spread(new[8:16])
    qf = new_y[0, 16:24] + jnp.where(half == 0, new_y[3, 16:24], new_y[1, 16:24])
    second = iota((8, 1), 0) >= 4
    s0 = jnp.sum(qf * key0, axis=1, keepdims=True) * SCALE
    s1 = jnp.where(second, jnp.sum(qf * key1, axis=1, keepdims=True) * SCALE, NEG)
    new_top = jnp.maximum(s0, s1)
    p0 = jnp.exp2(s0 - new_top)
    p1 = jnp.where(second, jnp.exp2(s1 - new_top), 0.0)
    new_total = p0 + p1
    new_out = p0 * val0 + p1 * val1
    new_out = jnp.where(half == 0, new_out, pltpu.roll(new_out, 64, 1))

    for pairs in back.values():
        for c in pairs:
            c.wait_recv()
    mls = [ml_xy[0]] + [ml_in[a, b] for a, b in others]
    mls = [jnp.where(pair == 0, m, pltpu.roll(m, 120, 1)) for m in mls]
    outs = [o_xy.at[0, y]] + [o_in.at[a, b] for a, b in others]
    top = functools.reduce(jnp.maximum, mls)
    factors = [jnp.exp2(m - top) for m in mls]
    total = sum(pltpu.roll(f, 64, 1) * m for f, m in zip(factors, mls))
    for j in range(2):
        rows = [o[16 * j : 16 * j + 16].astype(F32) for o in outs]
        for rh in range(2):
            i = j * 4 + rh
            acc = sum(
                jnp.where(lane < 64, f[:, i : i + 1], f[:, i + 2 : i + 3]) * o[8 * rh : 8 * rh + 8]
                for f, o in zip(factors, rows)
            )
            swapped = pltpu.roll(acc, 64, 1)
            ends = [jnp.where(lane < 96, top[:, k : k + 1], total[:, 64 + k : 65 + k]) for k in (i, i + 2)]
            low = jnp.where(lane < 64, acc, ends[0])
            high = jnp.where(lane < 64, swapped, ends[1])
            zz = j * 4 + rh * 2
            fin[zz] = jnp.where(row8 < 4, low, pltpu.roll(high, 4, 0))
            fin[zz + 1] = jnp.where(row8 < 4, pltpu.roll(low, 4, 0), high)

    own = fin[z]
    best = jnp.maximum(own[:, 64:65], new_top)
    new_tile = jnp.where(lane < 64, new_out, new_total)
    own = jnp.exp2(own[:, 64:65] - best) * own + jnp.exp2(new_top - best) * new_tile
    fin[z] = jnp.where((lane >= 64) & (lane < 96), best, own)

    f = []
    for d in (4, 3, 5, 2, 6, 1, 7, 0):
        for other in range(2):
            if d or other:
                i = other * NZ + d
                f.append(remote(fin.at[lax.rem(z + d, NZ)], fin_in.at[i], f_s.at[i], f_r.at[i], z_peer[other][d]))
                f[-1].start()
    for c in f:
        c.wait_recv()

    parts = []
    for other in range(2):
        tiles = [fin_in[other * NZ + d] if d or other else fin[z] for d in range(NZ)]
        top = functools.reduce(jnp.maximum, tiles)
        acc = sum(jnp.exp2(t - top)[:, 64:65] * t for t in tiles)
        parts.append(acc[:, :64] / acc[:, 96:97])
    row = iota((8, 64), 0)
    slot_row = jnp.zeros((8, 64), I32)
    for r in range(8):
        slot_row = jnp.where(row == r, slots[r], slot_row)
    for t in range(2):
        result = jnp.zeros((8, 64), F32)
        for other in range(2):
            group = core + other - 2 * core * other
            for s in range(SLOTS):
                i = t * 4 + s
                found = slot_row == group * SLOTS + s
                result = jnp.where(found, jnp.broadcast_to(parts[other][i : i + 1], (8, 64)), result)
        out_ref[t] = result.astype(BF16)

    for c in ny + nz + qz + qxy + [c for pairs in back.values() for c in pairs] + f:
        c.wait_send()


def local(queries, new_keys, new_values, key_cache, value_cache, lengths, row_slot):
    sem = pltpu.SemaphoreType.DMA
    return pl.pallas_call(
        kernel,
        out_shape=jax.ShapeDtypeStruct(queries.shape, BF16),
        in_specs=[pl.BlockSpec(memory_space=pltpu.HBM)] * 7,
        out_specs=pl.BlockSpec(memory_space=pltpu.VMEM),
        scratch_shapes=[
            pltpu.VMEM(queries.shape, BF16),
            pltpu.VMEM(new_keys.shape, BF16),
            pltpu.VMEM(new_values.shape, BF16),
            pltpu.SMEM(lengths.shape, I32),
            pltpu.SMEM(row_slot.shape, I32),
            pltpu.VMEM(key_cache.shape, BF16),
            pltpu.VMEM(value_cache.shape, BF16),
            pltpu.VMEM((NY, 24, 128), F32),
            pltpu.VMEM((4, 16, 128), F32),
            pltpu.VMEM((NZ, 4, 128), F32),
            pltpu.VMEM((NX, NY, 32, 128), BF16),
            pltpu.VMEM((NX, NY, 32, 128), BF16),
            pltpu.VMEM((NX, 8, 128), F32),
            pltpu.VMEM((NX, NY, 32, 128), BF16),
            pltpu.VMEM((NX, NY, 8, 128), F32),
            pltpu.VMEM((NZ, 8, 128), F32),
            pltpu.VMEM((2 * NZ, 8, 128), F32),
            sem((5,)), sem((2 * SLOTS,)),
            sem((NY,)), sem((NY,)), sem((4,)), sem((4,)), sem((NZ,)), sem((NZ,)),
            sem((NX, NY)), sem((NX, NY)), sem((NX, NY)), sem((NX, NY)), sem((NX, NY)), sem((NX, NY)),
            sem((2 * NZ,)), sem((2 * NZ,)),
        ],
        compiler_params=pltpu.CompilerParams(
            collective_id=0, has_side_effects=True, vmem_limit_bytes=64 * 1024 * 1024
        ),
    )(queries, new_keys, new_values, key_cache, value_cache, lengths, row_slot)


def solution(mesh):
    in_specs = (
        P(None, None, "seq"),
        P(None, None, "seq"),
        P(None, None, "seq"),
        P("rows", "seq", None),
        P("rows", "seq", None),
        P(),
        P(),
    )
    out_specs = P(None, None, "seq")
    return jax.shard_map(local, mesh=mesh, in_specs=in_specs, out_specs=out_specs, check_vma=False)
```

```python
import functools

import jax
import jax.numpy as jnp
from jax import lax
from jax.experimental import pallas as pl
from jax.experimental.pallas import tpu as pltpu
from jax.sharding import PartitionSpec as P

NX, NZ, NY = 4, 8, 4
HEAD_DIM = 128
SLOTS = 4
CTX = 256
NEG = -1e30
SCALE = HEAD_DIM**-0.5 * 1.4426950408889634
MESH = pl.DeviceIdType.MESH
F32, BF16, I32 = jnp.float32, jnp.bfloat16, jnp.int32


def iota(shape, dim):
    return lax.broadcasted_iota(I32, shape, dim)


def kernel(
    q_hbm, nk_hbm, nv_hbm, k_hbm, v_hbm, len_hbm, slot_hbm, out_ref,
    q_in, nk_in, nv_in, len_ref, slot_ref, k_buf, v_buf,
    new_y, new_z, q_z, q_xy, o_xy, ml_xy, o_in, ml_in, fin, fin_in,
    in_sem, cache_sem,
    ny_s, ny_r, nz_s, nz_r, qz_s, qz_r, qxy_s, qxy_r, o_s, o_r, ml_s, ml_r, f_s, f_r,
):
    seq, core = lax.axis_index("seq"), lax.axis_index("rows")
    y = lax.rem(seq, NY)
    z = lax.rem(lax.div(seq, NY), NZ)
    x = lax.div(seq, NY * NZ)
    pair, half = lax.div(y, 2), lax.rem(y, 2)
    zq = lax.rem(z, 4)

    def at(xx, zz, yy, cc):
        return {"seq": (xx * NZ + zz) * NY + yy, "rows": cc}

    def remote(src, dst, send, recv, target):
        return pltpu.make_async_remote_copy(
            src_ref=src, dst_ref=dst, send_sem=send, recv_sem=recv, device_id=target, device_id_type=MESH
        )

    z_peer = [[at(x, lax.rem(z + d, NZ), y, c) for d in range(NZ)] for c in (core, 1 - core)]
    xy_peer = [[at(lax.rem(x + a, NX), z, lax.rem(y + b, NY), core) for b in range(NY)] for a in range(NX)]
    half_peer = [at(x, z - zq + lax.rem(zq + d, 4), y, core) for d in range(4)]
    others = [(a, b) for a in range(NX) for b in range(NY) if a or b]

    loads = [
        pltpu.make_async_copy(q_hbm, q_in, in_sem.at[0]),
        pltpu.make_async_copy(slot_hbm, slot_ref, in_sem.at[1]),
        pltpu.make_async_copy(nk_hbm, nk_in, in_sem.at[2]),
        pltpu.make_async_copy(nv_hbm, nv_in, in_sem.at[3]),
        pltpu.make_async_copy(len_hbm, len_ref, in_sem.at[4]),
    ]
    for c in loads:
        c.start()

    barrier = pltpu.get_barrier_semaphore()
    peers = z_peer[0][1:] + z_peer[1] + [xy_peer[a][b] for a, b in others]
    for p in peers:
        pl.semaphore_signal(barrier, inc=1, device_id=p, device_id_type=MESH)

    k_loads = [pltpu.make_async_copy(k_hbm.at[s], k_buf.at[s], cache_sem.at[s]) for s in range(SLOTS)]
    v_loads = [pltpu.make_async_copy(v_hbm.at[s], v_buf.at[s], cache_sem.at[SLOTS + s]) for s in range(SLOTS)]
    for c in k_loads + v_loads:
        c.start()
    for c in loads:
        c.wait()
    slots = [slot_ref[r] for r in range(8)]

    def by_slot(ref):
        width = ref.shape[2]
        row = iota((8, width), 0)
        wanted = core * SLOTS + lax.rem(row, 4)
        acc = jnp.zeros((8, width), F32)
        for t in range(2):
            whole = ref[t].astype(F32)
            for r in range(8):
                hit = (wanted == slots[r]) & (lax.div(row, 4) == t)
                acc = jnp.where(hit, jnp.broadcast_to(whole[r : r + 1], (8, width)), acc)
        return acc

    lane, row8 = iota((8, 128), 1), iota((8, 128), 0)
    mine = by_slot(q_in)
    q_z[z] = jnp.concatenate([mine[0:4], mine[4:8]], axis=1)

    pl.semaphore_wait(barrier, len(peers))

    def qz_copy(d, origin):
        return remote(q_z.at[origin], q_z.at[origin], qz_s.at[d], qz_r.at[d], z_peer[0][d])

    qz = [qz_copy(d, z) for d in (4, 3, 5, 2, 6, 1, 7)]
    for c in qz:
        c.start()

    base = zq * 32 + y * 8
    for i, ref in enumerate((nk_in, nv_in)):
        part = by_slot(ref)
        acc = jnp.zeros((8, 128), F32)
        for f in range(8):
            acc = jnp.where(lane == base + f, jnp.broadcast_to(part[:, f : f + 1], (8, 128)), acc)
        new_y[0, 8 * i : 8 * i + 8] = acc
    new_y[0, 16:24] = jnp.where(lax.div(lane, 64) == half, jnp.concatenate([mine, mine], axis=1), 0.0)
    ny = [remote(new_y.at[0], new_y.at[d], ny_s.at[d], ny_r.at[d], xy_peer[0][d]) for d in range(1, NY)]
    for c in ny:
        c.start()

    slot_of = lax.rem(iota((64, CTX), 0), SLOTS)
    limit = jnp.zeros((64, CTX), I32)
    for s in range(SLOTS):
        n = jnp.int32(0)
        for r in range(8):
            n = n + jnp.where(slots[r] == core * SLOTS + s, len_ref[r], 0)
        limit = jnp.where(slot_of == s, n, limit)
    valid = seq * CTX + iota((64, CTX), 1) < limit
    slot_out = lax.rem(iota((64, HEAD_DIM), 0), SLOTS)
    left16, left32 = iota((16, 128), 1) < 64, iota((32, 128), 1) < 64

    for d in range(1, NZ):
        qz_copy(d, lax.rem(z + NZ - d, NZ)).wait_recv()
    q_xy[x, y] = jnp.concatenate([q_z[i] for i in range(NZ)], axis=0).astype(BF16)

    def qxy_copy(a, b, xx, yy):
        return remote(q_xy.at[xx, yy], q_xy.at[xx, yy], qxy_s.at[a, b], qxy_r.at[a, b], xy_peer[a][b])

    qxy = [qxy_copy(a, b, x, y) for a in (2, 1, 3, 0) for b in (2, 1, 3, 0) if a or b]
    for c in qxy:
        c.start()

    for c in ny:
        c.wait_recv()
    new_z[0] = (new_y[0, 0:16] + new_y[1, 0:16]) + (new_y[2, 0:16] + new_y[3, 0:16])
    nz = [remote(new_z.at[0], new_z.at[d], nz_s.at[d], nz_r.at[d], half_peer[d]) for d in range(1, 4)]
    for c in nz:
        c.start()

    for c in k_loads + v_loads:
        c.wait()

    def attend(xb, slot):
        turned = []
        for hh in range(2):
            a, b = q_xy[xb, 2 * hh].astype(F32), q_xy[xb, 2 * hh + 1].astype(F32)
            turned.append(jnp.where(left32, a, pltpu.roll(b, 64, 1)).astype(BF16))
            turned.append(jnp.where(left32, pltpu.roll(a, 64, 1), b).astype(BF16))
        ml = jnp.zeros((8, 128), F32)
        for j in range(2):
            cols = pl.ds(pl.multiple_of((xb * 2 + j) * HEAD_DIM, HEAD_DIM), HEAD_DIM)
            q = jnp.concatenate([u[16 * j : 16 * j + 16] for u in turned], axis=0)
            scores = None
            for s in range(SLOTS):
                part = lax.dot_general(q, k_buf[s, :, cols], (((1,), (1,)), ((), ())), preferred_element_type=F32)
                scores = part if s == 0 else jnp.where(slot_of == s, part, scores)
            scores = jnp.where(valid, scores * SCALE, NEG)
            top = jnp.max(scores, axis=1, keepdims=True)
            p = jnp.where(valid, jnp.exp2(scores - top), 0.0)
            total = jnp.sum(p, axis=1, keepdims=True)
            p = p.astype(BF16)
            out = None
            for s in range(SLOTS):
                part = jnp.dot(p, v_buf[s, :, cols], preferred_element_type=F32)
                out = part if s == 0 else jnp.where(slot_out == s, part, out)
            for hh in range(2):
                first, second = out[32 * hh : 32 * hh + 16], out[32 * hh + 16 : 32 * hh + 32]
                rows = slice(16 * j, 16 * j + 16)
                o_xy[slot, 2 * hh, rows] = jnp.where(left16, first, pltpu.roll(second, 64, 1)).astype(BF16)
                o_xy[slot, 2 * hh + 1, rows] = jnp.where(left16, pltpu.roll(first, 64, 1), second).astype(BF16)
                for t in range(2):
                    for rh in range(2):
                        here = slice(32 * hh + 16 * t + 8 * rh, 32 * hh + 16 * t + 8 * rh + 8)
                        i = hh * 8 + j * 4 + t * 2 + rh
                        ml = jnp.where(lane == i, top[here], ml)
                        ml = jnp.where(lane == 64 + i, total[here], ml)
        ml_xy[slot] = ml

    back = {}
    for a in range(NX):
        xb = lax.rem(x + NX - a, NX)
        for b in range(NY):
            if a or b:
                qxy_copy(a, b, xb, lax.rem(y + NY - b, NY)).wait_recv()
        attend(xb, a)
        for b in (2, 1, 3, 0):
            if a or b:
                target = xy_peer[(NX - a) % NX][b]
                yy = lax.rem(y + b, NY)
                back[a, b] = (
                    remote(o_xy.at[a, yy], o_in.at[a, b], o_s.at[a, b], o_r.at[a, b], target),
                    remote(ml_xy.at[a], ml_in.at[a, b], ml_s.at[a, b], ml_r.at[a, b], target),
                )
                for c in back[a, b]:
                    c.start()

    for c in nz:
        c.wait_recv()
    new = (new_z[0] + new_z[1]) + (new_z[2] + new_z[3])

    def spread(block):
        turned = jnp.concatenate([block[4:8], block[0:4]], axis=0)
        return jnp.where(row8 < 4, block, turned), jnp.where(row8 < 4, turned, block)

    key0, key1 = spread(new[0:8])
    val0, val1 = spread(new[8:16])
    qf = new_y[0, 16:24] + jnp.where(half == 0, new_y[3, 16:24], new_y[1, 16:24])
    second = iota((8, 1), 0) >= 4
    s0 = jnp.sum(qf * key0, axis=1, keepdims=True) * SCALE
    s1 = jnp.where(second, jnp.sum(qf * key1, axis=1, keepdims=True) * SCALE, NEG)
    new_top = jnp.maximum(s0, s1)
    p0 = jnp.exp2(s0 - new_top)
    p1 = jnp.where(second, jnp.exp2(s1 - new_top), 0.0)
    new_total = p0 + p1
    new_out = p0 * val0 + p1 * val1
    new_out = jnp.where(half == 0, new_out, pltpu.roll(new_out, 64, 1))

    for pairs in back.values():
        for c in pairs:
            c.wait_recv()
    mls = [ml_xy[0]] + [ml_in[a, b] for a, b in others]
    mls = [jnp.where(pair == 0, m, pltpu.roll(m, 120, 1)) for m in mls]
    outs = [o_xy.at[0, y]] + [o_in.at[a, b] for a, b in others]
    top = functools.reduce(jnp.maximum, mls)
    factors = [jnp.exp2(m - top) for m in mls]
    total = sum(pltpu.roll(f, 64, 1) * m for f, m in zip(factors, mls))
    for j in range(2):
        rows = [o[16 * j : 16 * j + 16].astype(F32) for o in outs]
        for rh in range(2):
            i = j * 4 + rh
            acc = sum(
                jnp.where(lane < 64, f[:, i : i + 1], f[:, i + 2 : i + 3]) * o[8 * rh : 8 * rh + 8]
                for f, o in zip(factors, rows)
            )
            swapped = pltpu.roll(acc, 64, 1)
            ends = [jnp.where(lane < 96, top[:, k : k + 1], total[:, 64 + k : 65 + k]) for k in (i, i + 2)]
            low = jnp.where(lane < 64, acc, ends[0])
            high = jnp.where(lane < 64, swapped, ends[1])
            zz = j * 4 + rh * 2
            fin[zz] = jnp.where(row8 < 4, low, pltpu.roll(high, 4, 0))
            fin[zz + 1] = jnp.where(row8 < 4, pltpu.roll(low, 4, 0), high)

    own = fin[z]
    best = jnp.maximum(own[:, 64:65], new_top)
    new_tile = jnp.where(lane < 64, new_out, new_total)
    own = jnp.exp2(own[:, 64:65] - best) * own + jnp.exp2(new_top - best) * new_tile
    fin[z] = jnp.where((lane >= 64) & (lane < 96), best, own)

    f = []
    for d in (4, 3, 5, 2, 6, 1, 7, 0):
        for other in range(2):
            if d or other:
                i = other * NZ + d
                f.append(remote(fin.at[lax.rem(z + d, NZ)], fin_in.at[i], f_s.at[i], f_r.at[i], z_peer[other][d]))
                f[-1].start()
    for c in f:
        c.wait_recv()

    parts = []
    for other in range(2):
        tiles = [fin_in[other * NZ + d] if d or other else fin[z] for d in range(NZ)]
        top = functools.reduce(jnp.maximum, tiles)
        acc = sum(jnp.exp2(t - top)[:, 64:65] * t for t in tiles)
        parts.append(acc[:, :64] / acc[:, 96:97])
    row = iota((8, 64), 0)
    slot_row = jnp.zeros((8, 64), I32)
    for r in range(8):
        slot_row = jnp.where(row == r, slots[r], slot_row)
    for t in range(2):
        result = jnp.zeros((8, 64), F32)
        for other in range(2):
            group = core + other - 2 * core * other
            for s in range(SLOTS):
                i = t * 4 + s
                found = slot_row == group * SLOTS + s
                result = jnp.where(found, jnp.broadcast_to(parts[other][i : i + 1], (8, 64)), result)
        out_ref[t] = result.astype(BF16)

    for c in ny + nz + qz + qxy + [c for pairs in back.values() for c in pairs] + f:
        c.wait_send()


def local(queries, new_keys, new_values, key_cache, value_cache, lengths, row_slot):
    sem = pltpu.SemaphoreType.DMA
    args = (queries, new_keys, new_values, key_cache, value_cache, lengths, row_slot)
    return pl.pallas_call(
        kernel,
        out_shape=jax.ShapeDtypeStruct(queries.shape, BF16),
        in_specs=[pl.BlockSpec(memory_space=pltpu.HBM)] * 7,
        out_specs=pl.BlockSpec(memory_space=pltpu.VMEM),
        scratch_shapes=[
            pltpu.VMEM(queries.shape, BF16),
            pltpu.VMEM(new_keys.shape, BF16),
            pltpu.VMEM(new_values.shape, BF16),
            pltpu.SMEM(lengths.shape, I32),
            pltpu.SMEM(row_slot.shape, I32),
            pltpu.VMEM(key_cache.shape, BF16),
            pltpu.VMEM(value_cache.shape, BF16),
            pltpu.VMEM((NY, 24, 128), F32),
            pltpu.VMEM((4, 16, 128), F32),
            pltpu.VMEM((NZ, 4, 128), F32),
            pltpu.VMEM((NX, NY, 32, 128), BF16),
            pltpu.VMEM((NX, NY, 32, 128), BF16),
            pltpu.VMEM((NX, 8, 128), F32),
            pltpu.VMEM((NX, NY, 32, 128), BF16),
            pltpu.VMEM((NX, NY, 8, 128), F32),
            pltpu.VMEM((NZ, 8, 128), F32),
            pltpu.VMEM((2 * NZ, 8, 128), F32),
            sem((5,)), sem((2 * SLOTS,)),
            sem((NY,)), sem((NY,)), sem((4,)), sem((4,)), sem((NZ,)), sem((NZ,)),
            sem((NX, NY)), sem((NX, NY)), sem((NX, NY)), sem((NX, NY)), sem((NX, NY)), sem((NX, NY)),
            sem((2 * NZ,)), sem((2 * NZ,)),
        ],
        compiler_params=pltpu.CompilerParams(
            collective_id=0, has_side_effects=True, vmem_limit_bytes=48 * 1024 * 1024
        ),
    )(*(pltpu.with_memory_space_constraint(a, pltpu.HBM) for a in args))


def solution(mesh):
    in_specs = (
        P(None, None, "seq"),
        P(None, None, "seq"),
        P(None, None, "seq"),
        P("rows", "seq", None),
        P("rows", "seq", None),
        P(),
        P(),
    )
    out_specs = P(None, None, "seq")
    return jax.shard_map(local, mesh=mesh, in_specs=in_specs, out_specs=out_specs, check_vma=False)
```

```python
import functools

import jax
import jax.numpy as jnp
from jax import lax
from jax.experimental import pallas as pl
from jax.experimental.pallas import tpu as pltpu
from jax.sharding import PartitionSpec as P

NX, NZ, NY = 4, 8, 4
HEAD_DIM = 128
SLOTS = 4
CTX = 256
NEG = -1e30
SCALE = HEAD_DIM**-0.5 * 1.4426950408889634
MESH = pl.DeviceIdType.MESH
F32, BF16, I32 = jnp.float32, jnp.bfloat16, jnp.int32


def iota(shape, dim):
    return lax.broadcasted_iota(I32, shape, dim)


def kernel(
    q_hbm, nk_hbm, nv_hbm, k_hbm, v_hbm, len_hbm, slot_hbm, out_ref,
    q_in, nk_in, nv_in, len_ref, slot_ref, k_buf, v_buf,
    new_y, new_z, new_tile, q_z, q_xy, o_xy, ml_xy, o_in, ml_in, fin, fin_in,
    in_sem, cache_sem,
    ny_s, ny_r, nz_s, nz_r, nc_s, nc_r, qz_s, qz_r, qxy_s, qxy_r, o_s, o_r, ml_s, ml_r, f_s, f_r,
):
    seq, core = lax.axis_index("seq"), lax.axis_index("rows")
    y = lax.rem(seq, NY)
    z = lax.rem(lax.div(seq, NY), NZ)
    x = lax.div(seq, NY * NZ)
    pair, half = lax.div(y, 2), lax.rem(y, 2)
    zq = lax.rem(z, 4)

    def at(xx, zz, yy, cc):
        return {"seq": (xx * NZ + zz) * NY + yy, "rows": cc}

    def remote(src, dst, send, recv, target):
        return pltpu.make_async_remote_copy(
            src_ref=src, dst_ref=dst, send_sem=send, recv_sem=recv, device_id=target, device_id_type=MESH
        )

    z_peer = [[at(x, lax.rem(z + d, NZ), y, c) for d in range(NZ)] for c in (core, 1 - core)]
    xy_peer = [[at(lax.rem(x + a, NX), z, lax.rem(y + b, NY), core) for b in range(NY)] for a in range(NX)]
    half_peer = [at(x, z - zq + lax.rem(zq + d, 4), y, core) for d in range(4)]
    others = [(a, b) for a in range(NX) for b in range(NY) if a or b]

    loads = [
        pltpu.make_async_copy(q_hbm, q_in, in_sem.at[0]),
        pltpu.make_async_copy(slot_hbm, slot_ref, in_sem.at[1]),
        pltpu.make_async_copy(nk_hbm, nk_in, in_sem.at[2]),
        pltpu.make_async_copy(nv_hbm, nv_in, in_sem.at[3]),
        pltpu.make_async_copy(len_hbm, len_ref, in_sem.at[4]),
    ]
    for c in loads:
        c.start()

    barrier = pltpu.get_barrier_semaphore()
    peers = z_peer[0][1:] + z_peer[1] + [xy_peer[a][b] for a, b in others]
    for p in peers:
        pl.semaphore_signal(barrier, inc=1, device_id=p, device_id_type=MESH)

    k_loads = [pltpu.make_async_copy(k_hbm.at[s], k_buf.at[s], cache_sem.at[s]) for s in range(SLOTS)]
    v_loads = [pltpu.make_async_copy(v_hbm.at[s], v_buf.at[s], cache_sem.at[SLOTS + s]) for s in range(SLOTS)]
    for c in k_loads + v_loads:
        c.start()
    for c in loads:
        c.wait()
    slots = [slot_ref[r] for r in range(8)]

    def by_slot(ref):
        width = ref.shape[2]
        row = iota((8, width), 0)
        wanted = core * SLOTS + lax.rem(row, 4)
        acc = jnp.zeros((8, width), F32)
        for t in range(2):
            whole = ref[t].astype(F32)
            for r in range(8):
                hit = (wanted == slots[r]) & (lax.div(row, 4) == t)
                acc = jnp.where(hit, jnp.broadcast_to(whole[r : r + 1], (8, width)), acc)
        return acc

    lane, row8 = iota((8, 128), 1), iota((8, 128), 0)
    mine = by_slot(q_in)
    q_z[z] = jnp.concatenate([mine[0:4], mine[4:8]], axis=1)

    pl.semaphore_wait(barrier, len(peers))

    def qz_copy(d, origin):
        return remote(q_z.at[origin], q_z.at[origin], qz_s.at[d], qz_r.at[d], z_peer[0][d])

    qz = [qz_copy(d, z) for d in (4, 3, 5, 2, 6, 1, 7)]
    for c in qz:
        c.start()

    base = zq * 32 + y * 8
    for i, ref in enumerate((nk_in, nv_in)):
        part = by_slot(ref)
        acc = jnp.zeros((8, 128), F32)
        for f in range(8):
            acc = jnp.where(lane == base + f, jnp.broadcast_to(part[:, f : f + 1], (8, 128)), acc)
        new_y[0, 8 * i : 8 * i + 8] = acc
    new_y[0, 16:24] = jnp.where(lax.div(lane, 64) == half, jnp.concatenate([mine, mine], axis=1), 0.0)
    ny = [remote(new_y.at[0], new_y.at[d], ny_s.at[d], ny_r.at[d], xy_peer[0][d]) for d in range(1, NY)]
    for c in ny:
        c.start()

    slot_of = lax.rem(iota((128, CTX), 0), SLOTS)
    limit = jnp.zeros((128, CTX), I32)
    for s in range(SLOTS):
        n = jnp.int32(0)
        for r in range(8):
            n = n + jnp.where(slots[r] == core * SLOTS + s, len_ref[r], 0)
        limit = jnp.where(slot_of == s, n, limit)
    valid = seq * CTX + iota((128, CTX), 1) < limit
    left16, left32 = iota((16, 128), 1) < 64, iota((32, 128), 1) < 64

    for d in range(1, NZ):
        qz_copy(d, lax.rem(z + NZ - d, NZ)).wait_recv()
    q_xy[x, y] = jnp.concatenate([q_z[i] for i in range(NZ)], axis=0).astype(BF16)

    def qxy_copy(a, b, xx, yy):
        return remote(q_xy.at[xx, yy], q_xy.at[xx, yy], qxy_s.at[a, b], qxy_r.at[a, b], xy_peer[a][b])

    qxy = [qxy_copy(a, b, x, y) for a in (2, 1, 3, 0) for b in (2, 1, 3, 0) if a or b]
    for c in qxy:
        c.start()

    for c in ny:
        c.wait_recv()
    new_z[0] = (new_y[0, 0:16] + new_y[1, 0:16]) + (new_y[2, 0:16] + new_y[3, 0:16])
    nz = [remote(new_z.at[0], new_z.at[d], nz_s.at[d], nz_r.at[d], half_peer[d]) for d in range(1, 4)]
    for c in nz:
        c.start()

    for c in k_loads + v_loads:
        c.wait()

    def attend(xb, slot):
        turned = []
        for hh in range(2):
            a, b = q_xy[xb, 2 * hh].astype(F32), q_xy[xb, 2 * hh + 1].astype(F32)
            turned.append(jnp.where(left32, a, pltpu.roll(b, 64, 1)).astype(BF16))
            turned.append(jnp.where(left32, pltpu.roll(a, 64, 1), b).astype(BF16))
        cols = pl.ds(pl.multiple_of(xb * 2 * HEAD_DIM, 2 * HEAD_DIM), 2 * HEAD_DIM)
        none = jnp.zeros((64, HEAD_DIM), BF16)
        q0, q1 = (jnp.concatenate([u[16 * j : 16 * j + 16] for u in turned], axis=0) for j in range(2))
        q = jnp.concatenate(
            [jnp.concatenate([q0, none], axis=1), jnp.concatenate([none, q1], axis=1)], axis=0
        )
        scores = None
        for s in range(SLOTS):
            part = lax.dot_general(q, k_buf[s, :, cols], (((1,), (1,)), ((), ())), preferred_element_type=F32)
            scores = part if s == 0 else jnp.where(slot_of == s, part, scores)
        scores = jnp.where(valid, scores * SCALE, NEG)
        top = jnp.maximum(jnp.max(scores, axis=1, keepdims=True), NEG / 2)
        p = jnp.exp2(scores - top)
        total = jnp.sum(p, axis=1, keepdims=True)
        p = p.astype(BF16)
        sums = None
        for s in range(SLOTS):
            part = jnp.dot(p, v_buf[s, :, cols], preferred_element_type=F32)
            sums = part if s == 0 else jnp.where(slot_of == s, part, sums)
        ml = jnp.zeros((8, 128), F32)
        for j in range(2):
            out = sums[64 * j : 64 * j + 64, HEAD_DIM * j : HEAD_DIM * j + HEAD_DIM]
            for hh in range(2):
                first, second = out[32 * hh : 32 * hh + 16], out[32 * hh + 16 : 32 * hh + 32]
                rows = slice(16 * j, 16 * j + 16)
                o_xy[slot, 2 * hh, rows] = jnp.where(left16, first, pltpu.roll(second, 64, 1)).astype(BF16)
                o_xy[slot, 2 * hh + 1, rows] = jnp.where(left16, pltpu.roll(first, 64, 1), second).astype(BF16)
                for t in range(2):
                    for rh in range(2):
                        start = 64 * j + 32 * hh + 16 * t + 8 * rh
                        here = slice(start, start + 8)
                        i = hh * 8 + j * 4 + t * 2 + rh
                        ml = jnp.where(lane == i, top[here], ml)
                        ml = jnp.where(lane == 64 + i, total[here], ml)
        ml_xy[slot] = ml

    back = {}
    for a in range(NX):
        xb = lax.rem(x + NX - a, NX)
        for b in range(NY):
            if a or b:
                qxy_copy(a, b, xb, lax.rem(y + NY - b, NY)).wait_recv()
        attend(xb, a)
        for b in (2, 1, 3, 0):
            if a or b:
                target = xy_peer[(NX - a) % NX][b]
                yy = lax.rem(y + b, NY)
                back[a, b] = (
                    remote(o_xy.at[a, yy], o_in.at[a, b], o_s.at[a, b], o_r.at[a, b], target),
                    remote(ml_xy.at[a], ml_in.at[a, b], ml_s.at[a, b], ml_r.at[a, b], target),
                )
                for c in back[a, b]:
                    c.start()

    for c in nz:
        c.wait_recv()
    new = (new_z[0] + new_z[1]) + (new_z[2] + new_z[3])

    def spread(block):
        turned = jnp.concatenate([block[4:8], block[0:4]], axis=0)
        return jnp.where(row8 < 4, block, turned), jnp.where(row8 < 4, turned, block)

    key0, key1 = spread(new[0:8])
    val0, val1 = spread(new[8:16])
    qf = new_y[0, 16:24] + jnp.where(half == 0, new_y[3, 16:24], new_y[1, 16:24])
    second = iota((8, 1), 0) >= 4
    s0 = jnp.sum(qf * key0, axis=1, keepdims=True) * SCALE
    s1 = jnp.where(second, jnp.sum(qf * key1, axis=1, keepdims=True) * SCALE, NEG)
    new_top = jnp.maximum(s0, s1)
    p0 = jnp.exp2(s0 - new_top)
    p1 = jnp.where(second, jnp.exp2(s1 - new_top), 0.0)
    new_total = p0 + p1
    new_out = p0 * val0 + p1 * val1
    new_out = jnp.where(half == 0, new_out, pltpu.roll(new_out, 64, 1))
    new_tile[0] = jnp.where(lane < 64, new_out, jnp.where(lane < 96, new_top, new_total))
    nc = remote(new_tile.at[0], new_tile.at[1], nc_s, nc_r, z_peer[1][0])
    nc.start()

    for pairs in back.values():
        for c in pairs:
            c.wait_recv()
    mls = [ml_xy[0]] + [ml_in[a, b] for a, b in others]
    mls = [jnp.where(pair == 0, m, pltpu.roll(m, 120, 1)) for m in mls]
    outs = [o_xy.at[0, y]] + [o_in.at[a, b] for a, b in others]
    top = functools.reduce(jnp.maximum, mls)
    factors = [jnp.exp2(m - top) for m in mls]
    total = sum(pltpu.roll(f, 64, 1) * m for f, m in zip(factors, mls))
    for j in range(2):
        rows = [o[16 * j : 16 * j + 16].astype(F32) for o in outs]
        for rh in range(2):
            i = j * 4 + rh
            acc = sum(
                jnp.where(lane < 64, f[:, i : i + 1], f[:, i + 2 : i + 3]) * o[8 * rh : 8 * rh + 8]
                for f, o in zip(factors, rows)
            )
            swapped = pltpu.roll(acc, 64, 1)
            ends = [jnp.where(lane < 96, top[:, k : k + 1], total[:, 64 + k : 65 + k]) for k in (i, i + 2)]
            low = jnp.where(lane < 64, acc, ends[0])
            high = jnp.where(lane < 64, swapped, ends[1])
            zz = j * 4 + rh * 2
            fin[zz] = jnp.where(row8 < 4, low, pltpu.roll(high, 4, 0))
            fin[zz + 1] = jnp.where(row8 < 4, pltpu.roll(low, 4, 0), high)

    f = []
    for d in (4, 3, 5, 2, 6, 1, 7, 0):
        for other in range(2):
            if d or other:
                i = other * NZ + d
                f.append(remote(fin.at[lax.rem(z + d, NZ)], fin_in.at[i], f_s.at[i], f_r.at[i], z_peer[other][d]))
                f[-1].start()
    for c in [nc] + f:
        c.wait_recv()

    parts = []
    for other in range(2):
        tiles = [fin_in[other * NZ + d] if d or other else fin[z] for d in range(NZ)] + [new_tile[other]]
        top = functools.reduce(jnp.maximum, tiles)
        acc = sum(jnp.exp2(t - top)[:, 64:65] * t for t in tiles)
        parts.append(acc[:, :64] / acc[:, 96:97])
    row = iota((8, 64), 0)
    slot_row = jnp.zeros((8, 64), I32)
    for r in range(8):
        slot_row = jnp.where(row == r, slots[r], slot_row)
    for t in range(2):
        result = jnp.zeros((8, 64), F32)
        for other in range(2):
            group = core + other - 2 * core * other
            for s in range(SLOTS):
                i = t * 4 + s
                found = slot_row == group * SLOTS + s
                result = jnp.where(found, jnp.broadcast_to(parts[other][i : i + 1], (8, 64)), result)
        out_ref[t] = result.astype(BF16)

    for c in [nc] + ny + nz + qz + qxy + [c for pairs in back.values() for c in pairs] + f:
        c.wait_send()


def local(queries, new_keys, new_values, key_cache, value_cache, lengths, row_slot):
    sem = pltpu.SemaphoreType.DMA
    args = (queries, new_keys, new_values, key_cache, value_cache, lengths, row_slot)
    return pl.pallas_call(
        kernel,
        out_shape=jax.ShapeDtypeStruct(queries.shape, BF16),
        in_specs=[pl.BlockSpec(memory_space=pltpu.HBM)] * 7,
        out_specs=pl.BlockSpec(memory_space=pltpu.VMEM),
        scratch_shapes=[
            pltpu.VMEM(queries.shape, BF16),
            pltpu.VMEM(new_keys.shape, BF16),
            pltpu.VMEM(new_values.shape, BF16),
            pltpu.SMEM(lengths.shape, I32),
            pltpu.SMEM(row_slot.shape, I32),
            pltpu.VMEM(key_cache.shape, BF16),
            pltpu.VMEM(value_cache.shape, BF16),
            pltpu.VMEM((NY, 24, 128), F32),
            pltpu.VMEM((4, 16, 128), F32),
            pltpu.VMEM((2, 8, 128), F32),
            pltpu.VMEM((NZ, 4, 128), F32),
            pltpu.VMEM((NX, NY, 32, 128), BF16),
            pltpu.VMEM((NX, NY, 32, 128), BF16),
            pltpu.VMEM((NX, 8, 128), F32),
            pltpu.VMEM((NX, NY, 32, 128), BF16),
            pltpu.VMEM((NX, NY, 8, 128), F32),
            pltpu.VMEM((NZ, 8, 128), F32),
            pltpu.VMEM((2 * NZ, 8, 128), F32),
            sem((5,)), sem((2 * SLOTS,)),
            sem((NY,)), sem((NY,)), sem((4,)), sem((4,)), sem, sem, sem((NZ,)), sem((NZ,)),
            sem((NX, NY)), sem((NX, NY)), sem((NX, NY)), sem((NX, NY)), sem((NX, NY)), sem((NX, NY)),
            sem((2 * NZ,)), sem((2 * NZ,)),
        ],
        compiler_params=pltpu.CompilerParams(
            collective_id=0, has_side_effects=True, vmem_limit_bytes=48 * 1024 * 1024
        ),
    )(*(pltpu.with_memory_space_constraint(a, pltpu.HBM) for a in args))


def solution(mesh):
    in_specs = (
        P(None, None, "seq"),
        P(None, None, "seq"),
        P(None, None, "seq"),
        P("rows", "seq", None),
        P("rows", "seq", None),
        P(),
        P(),
    )
    out_specs = P(None, None, "seq")
    return jax.shard_map(local, mesh=mesh, in_specs=in_specs, out_specs=out_specs, check_vma=False)
```

```python
import functools

import jax
import jax.numpy as jnp
from jax import lax
from jax.experimental import pallas as pl
from jax.experimental.pallas import tpu as pltpu
from jax.sharding import PartitionSpec as P

NX, NZ, NY = 4, 8, 4
HEAD_DIM = 128
SLOTS = 4
CTX = 256
NEG = -1e30
SCALE = HEAD_DIM**-0.5 * 1.4426950408889634
MESH = pl.DeviceIdType.MESH
F32, BF16, I32 = jnp.float32, jnp.bfloat16, jnp.int32


def iota(shape, dim):
    return lax.broadcasted_iota(I32, shape, dim)


def kernel(
    q_hbm, nk_hbm, nv_hbm, k_hbm, v_hbm, len_hbm, slot_hbm, out_ref,
    q_in, nk_in, nv_in, len_ref, slot_ref, k_buf, v_buf,
    new_y, new_z, new_tile, q_z, q_xy, o_xy, ml_xy, o_in, ml_in, fin, fin_in,
    in_sem, cache_sem,
    ny_s, ny_r, nz_s, nz_r, nc_s, nc_r, qz_s, qz_r, qxy_s, qxy_r, o_s, o_r, ml_s, ml_r, f_s, f_r,
):
    seq, core = lax.axis_index("seq"), lax.axis_index("rows")
    y = lax.rem(seq, NY)
    z = lax.rem(lax.div(seq, NY), NZ)
    x = lax.div(seq, NY * NZ)
    pair, half = lax.div(y, 2), lax.rem(y, 2)
    zq = lax.rem(z, 4)

    def at(xx, zz, yy, cc):
        return {"seq": (xx * NZ + zz) * NY + yy, "rows": cc}

    def remote(src, dst, send, recv, target):
        return pltpu.make_async_remote_copy(
            src_ref=src, dst_ref=dst, send_sem=send, recv_sem=recv, device_id=target, device_id_type=MESH
        )

    z_peer = [[at(x, lax.rem(z + d, NZ), y, c) for d in range(NZ)] for c in (core, 1 - core)]
    xy_peer = [[at(lax.rem(x + a, NX), z, lax.rem(y + b, NY), core) for b in range(NY)] for a in range(NX)]
    half_peer = [at(x, z - zq + lax.rem(zq + d, 4), y, core) for d in range(4)]
    others = [(a, b) for a in range(NX) for b in range(NY) if a or b]

    barrier = pltpu.get_barrier_semaphore()
    far = (4, 3, 5, 2, 6, 1, 7)
    peers = [z_peer[i][d] for d in far for i in (1, 0)] + [xy_peer[a][b] for a in (2, 1, 3, 0) for b in (2, 1, 3, 0) if a or b] + [z_peer[1][0]]
    for p in peers:
        pl.semaphore_signal(barrier, inc=1, device_id=p, device_id_type=MESH)

    loads = [
        pltpu.make_async_copy(q_hbm, q_in, in_sem.at[0]),
        pltpu.make_async_copy(slot_hbm, slot_ref, in_sem.at[1]),
        pltpu.make_async_copy(nk_hbm, nk_in, in_sem.at[2]),
        pltpu.make_async_copy(nv_hbm, nv_in, in_sem.at[3]),
        pltpu.make_async_copy(len_hbm, len_ref, in_sem.at[4]),
    ]
    for c in loads:
        c.start()

    k_loads = [pltpu.make_async_copy(k_hbm.at[s], k_buf.at[s], cache_sem.at[s]) for s in range(SLOTS)]
    v_loads = [pltpu.make_async_copy(v_hbm.at[s], v_buf.at[s], cache_sem.at[SLOTS + s]) for s in range(SLOTS)]
    for c in k_loads + v_loads:
        c.start()
    for c in loads:
        c.wait()
    slots = [slot_ref[r] for r in range(8)]

    def by_slot(ref):
        width = ref.shape[2]
        row = iota((8, width), 0)
        wanted = core * SLOTS + lax.rem(row, 4)
        acc = jnp.zeros((8, width), F32)
        for t in range(2):
            whole = ref[t].astype(F32)
            for r in range(8):
                hit = (wanted == slots[r]) & (lax.div(row, 4) == t)
                acc = jnp.where(hit, jnp.broadcast_to(whole[r : r + 1], (8, width)), acc)
        return acc

    lane, row8 = iota((8, 128), 1), iota((8, 128), 0)
    mine = by_slot(q_in)
    q_z[z] = jnp.concatenate([mine[0:4], mine[4:8]], axis=1)

    pl.semaphore_wait(barrier, len(peers))

    def qz_copy(d, origin):
        return remote(q_z.at[origin], q_z.at[origin], qz_s.at[d], qz_r.at[d], z_peer[0][d])

    qz = [qz_copy(d, z) for d in (4, 3, 5, 2, 6, 1, 7)]
    for c in qz:
        c.start()

    base = zq * 32 + y * 8
    for i, ref in enumerate((nk_in, nv_in)):
        part = by_slot(ref)
        acc = jnp.zeros((8, 128), F32)
        for f in range(8):
            acc = jnp.where(lane == base + f, jnp.broadcast_to(part[:, f : f + 1], (8, 128)), acc)
        new_y[0, 8 * i : 8 * i + 8] = acc
    new_y[0, 16:24] = jnp.where(lax.div(lane, 64) == half, jnp.concatenate([mine, mine], axis=1), 0.0)
    ny = [remote(new_y.at[0], new_y.at[d], ny_s.at[d], ny_r.at[d], xy_peer[0][d]) for d in range(1, NY)]
    for c in ny:
        c.start()

    slot_of = lax.rem(iota((128, CTX), 0), SLOTS)
    limit = jnp.zeros((128, CTX), I32)
    for s in range(SLOTS):
        n = jnp.int32(0)
        for r in range(8):
            n = n + jnp.where(slots[r] == core * SLOTS + s, len_ref[r], 0)
        limit = jnp.where(slot_of == s, n, limit)
    valid = seq * CTX + iota((128, CTX), 1) < limit
    left16, left32 = iota((16, 128), 1) < 64, iota((32, 128), 1) < 64

    for d in range(1, NZ):
        qz_copy(d, lax.rem(z + NZ - d, NZ)).wait_recv()
    q_xy[x, y] = jnp.concatenate([q_z[i] for i in range(NZ)], axis=0).astype(BF16)

    def qxy_copy(a, b, xx, yy):
        return remote(q_xy.at[xx, yy], q_xy.at[xx, yy], qxy_s.at[a, b], qxy_r.at[a, b], xy_peer[a][b])

    qxy = [qxy_copy(a, b, x, y) for a in (2, 1, 3, 0) for b in (2, 1, 3, 0) if a or b]
    for c in qxy:
        c.start()

    for c in ny:
        c.wait_recv()
    new_z[0] = (new_y[0, 0:16] + new_y[1, 0:16]) + (new_y[2, 0:16] + new_y[3, 0:16])
    nz = [remote(new_z.at[0], new_z.at[d], nz_s.at[d], nz_r.at[d], half_peer[d]) for d in range(1, 4)]
    for c in nz:
        c.start()

    for c in k_loads + v_loads:
        c.wait()

    def attend(xb, slot):
        turned = []
        for hh in range(2):
            a, b = q_xy[xb, 2 * hh].astype(F32), q_xy[xb, 2 * hh + 1].astype(F32)
            turned.append(jnp.where(left32, a, pltpu.roll(b, 64, 1)).astype(BF16))
            turned.append(jnp.where(left32, pltpu.roll(a, 64, 1), b).astype(BF16))
        cols = pl.ds(pl.multiple_of(xb * 2 * HEAD_DIM, 2 * HEAD_DIM), 2 * HEAD_DIM)
        none = jnp.zeros((64, HEAD_DIM), BF16)
        q0, q1 = (jnp.concatenate([u[16 * j : 16 * j + 16] for u in turned], axis=0) for j in range(2))
        q = jnp.concatenate(
            [jnp.concatenate([q0, none], axis=1), jnp.concatenate([none, q1], axis=1)], axis=0
        )
        scores = None
        for s in range(SLOTS):
            part = lax.dot_general(q, k_buf[s, :, cols], (((1,), (1,)), ((), ())), preferred_element_type=F32)
            scores = part if s == 0 else jnp.where(slot_of == s, part, scores)
        scores = jnp.where(valid, scores * SCALE, NEG)
        top = jnp.maximum(jnp.max(scores, axis=1, keepdims=True), NEG / 2)
        p = jnp.exp2(scores - top)
        total = jnp.sum(p, axis=1, keepdims=True)
        p = p.astype(BF16)
        sums = None
        for s in range(SLOTS):
            part = jnp.dot(p, v_buf[s, :, cols], preferred_element_type=F32)
            sums = part if s == 0 else jnp.where(slot_of == s, part, sums)
        ml = jnp.zeros((8, 128), F32)
        for j in range(2):
            out = sums[64 * j : 64 * j + 64, HEAD_DIM * j : HEAD_DIM * j + HEAD_DIM]
            for hh in range(2):
                first, second = out[32 * hh : 32 * hh + 16], out[32 * hh + 16 : 32 * hh + 32]
                rows = slice(16 * j, 16 * j + 16)
                o_xy[slot, 2 * hh, rows] = jnp.where(left16, first, pltpu.roll(second, 64, 1)).astype(BF16)
                o_xy[slot, 2 * hh + 1, rows] = jnp.where(left16, pltpu.roll(first, 64, 1), second).astype(BF16)
                for t in range(2):
                    for rh in range(2):
                        start = 64 * j + 32 * hh + 16 * t + 8 * rh
                        here = slice(start, start + 8)
                        i = hh * 8 + j * 4 + t * 2 + rh
                        ml = jnp.where(lane == i, top[here], ml)
                        ml = jnp.where(lane == 64 + i, total[here], ml)
        ml_xy[slot] = ml

    back = {}
    for a in range(NX):
        xb = lax.rem(x + NX - a, NX)
        for b in range(NY):
            if a or b:
                qxy_copy(a, b, xb, lax.rem(y + NY - b, NY)).wait_recv()
        attend(xb, a)
        for b in (2, 1, 3, 0):
            if a or b:
                target = xy_peer[(NX - a) % NX][b]
                yy = lax.rem(y + b, NY)
                back[a, b] = (
                    remote(ml_xy.at[a], ml_in.at[a, b], ml_s.at[a, b], ml_r.at[a, b], target),
                    remote(o_xy.at[a, yy], o_in.at[a, b], o_s.at[a, b], o_r.at[a, b], target),
                )
                for c in back[a, b]:
                    c.start()

    for c in nz:
        c.wait_recv()
    new = (new_z[0] + new_z[1]) + (new_z[2] + new_z[3])

    def spread(block):
        turned = jnp.concatenate([block[4:8], block[0:4]], axis=0)
        return jnp.where(row8 < 4, block, turned), jnp.where(row8 < 4, turned, block)

    key0, key1 = spread(new[0:8])
    val0, val1 = spread(new[8:16])
    qf = new_y[0, 16:24] + jnp.where(half == 0, new_y[3, 16:24], new_y[1, 16:24])
    second = iota((8, 1), 0) >= 4
    s0 = jnp.sum(qf * key0, axis=1, keepdims=True) * SCALE
    s1 = jnp.where(second, jnp.sum(qf * key1, axis=1, keepdims=True) * SCALE, NEG)
    new_top = jnp.maximum(s0, s1)
    p0 = jnp.exp2(s0 - new_top)
    p1 = jnp.where(second, jnp.exp2(s1 - new_top), 0.0)
    new_total = p0 + p1
    new_out = p0 * val0 + p1 * val1
    new_out = jnp.where(half == 0, new_out, pltpu.roll(new_out, 64, 1))
    new_tile[0] = jnp.where(lane < 64, new_out, jnp.where(lane < 96, new_top, new_total))
    nc = remote(new_tile.at[0], new_tile.at[1], nc_s, nc_r, z_peer[1][0])
    nc.start()

    def by_lane(tile, i):
        return jnp.where(lane < 64, tile[:, i : i + 1], tile[:, i + 2 : i + 3])

    def gathered(group):
        keys = [(a, b) for a in group for b in range(NY)]
        for i in range(2):
            for key in keys:
                if key in back:
                    back[key][i].wait_recv()
        mls = [ml_in[a, b] if a or b else ml_xy[0] for a, b in keys]
        mls = [jnp.where(pair == 0, m, pltpu.roll(m, 120, 1)) for m in mls]
        outs = [o_in.at[a, b] if a or b else o_xy.at[0, y] for a, b in keys]
        top = functools.reduce(jnp.maximum, mls)
        factors = [jnp.exp2(m - top) for m in mls]
        total = sum(pltpu.roll(f, 64, 1) * m for f, m in zip(factors, mls))
        sums = []
        for j in range(2):
            rows = [o[16 * j : 16 * j + 16].astype(F32) for o in outs]
            for rh in range(2):
                sums.append(sum(by_lane(f, j * 4 + rh) * o[8 * rh : 8 * rh + 8] for f, o in zip(factors, rows)))
        return top, total, sums

    early, late = gathered((0, 1)), gathered((2, 3))
    top = jnp.maximum(early[0], late[0])
    factors = [jnp.exp2(g[0] - top) for g in (early, late)]
    total = sum(pltpu.roll(f, 64, 1) * g[1] for f, g in zip(factors, (early, late)))
    for j in range(2):
        for rh in range(2):
            i = j * 4 + rh
            acc = sum(by_lane(f, i) * g[2][2 * j + rh] for f, g in zip(factors, (early, late)))
            swapped = pltpu.roll(acc, 64, 1)
            ends = [jnp.where(lane < 96, top[:, k : k + 1], total[:, 64 + k : 65 + k]) for k in (i, i + 2)]
            low = jnp.where(lane < 64, acc, ends[0])
            high = jnp.where(lane < 64, swapped, ends[1])
            zz = j * 4 + rh * 2
            fin[zz] = jnp.where(row8 < 4, low, pltpu.roll(high, 4, 0))
            fin[zz + 1] = jnp.where(row8 < 4, pltpu.roll(low, 4, 0), high)

    f = []
    for d in (4, 3, 5, 2, 6, 1, 7, 0):
        for other in range(2):
            if d or other:
                i = other * NZ + d
                f.append(remote(fin.at[lax.rem(z + d, NZ)], fin_in.at[i], f_s.at[i], f_r.at[i], z_peer[other][d]))
                f[-1].start()
    row = iota((8, 64), 0)
    slot_row = jnp.zeros((8, 64), I32)
    for r in range(8):
        slot_row = jnp.where(row == r, slots[r], slot_row)
    for c in [nc] + ny + nz + qz + qxy + [c for pairs in back.values() for c in pairs]:
        c.wait_send()
    for c in [nc] + f:
        c.wait_recv()

    parts = []
    for other in range(2):
        tiles = [fin_in[other * NZ + d] if d or other else fin[z] for d in range(NZ)] + [new_tile[other]]
        top = functools.reduce(jnp.maximum, tiles)
        acc = sum(jnp.exp2(t - top)[:, 64:65] * t for t in tiles)
        parts.append(acc[:, :64] / acc[:, 96:97])
    for t in range(2):
        result = jnp.zeros((8, 64), F32)
        for other in range(2):
            group = core + other - 2 * core * other
            for s in range(SLOTS):
                i = t * 4 + s
                found = slot_row == group * SLOTS + s
                result = jnp.where(found, jnp.broadcast_to(parts[other][i : i + 1], (8, 64)), result)
        out_ref[t] = result.astype(BF16)

    for c in f:
        c.wait_send()


def local(queries, new_keys, new_values, key_cache, value_cache, lengths, row_slot):
    sem = pltpu.SemaphoreType.DMA
    args = (queries, new_keys, new_values, key_cache, value_cache, lengths, row_slot)
    return pl.pallas_call(
        kernel,
        out_shape=jax.ShapeDtypeStruct(queries.shape, BF16),
        in_specs=[pl.BlockSpec(memory_space=pltpu.HBM)] * 7,
        out_specs=pl.BlockSpec(memory_space=pltpu.VMEM),
        scratch_shapes=[
            pltpu.VMEM(queries.shape, BF16),
            pltpu.VMEM(new_keys.shape, BF16),
            pltpu.VMEM(new_values.shape, BF16),
            pltpu.SMEM(lengths.shape, I32),
            pltpu.SMEM(row_slot.shape, I32),
            pltpu.VMEM(key_cache.shape, BF16),
            pltpu.VMEM(value_cache.shape, BF16),
            pltpu.VMEM((NY, 24, 128), F32),
            pltpu.VMEM((4, 16, 128), F32),
            pltpu.VMEM((2, 8, 128), F32),
            pltpu.VMEM((NZ, 4, 128), F32),
            pltpu.VMEM((NX, NY, 32, 128), BF16),
            pltpu.VMEM((NX, NY, 32, 128), BF16),
            pltpu.VMEM((NX, 8, 128), F32),
            pltpu.VMEM((NX, NY, 32, 128), BF16),
            pltpu.VMEM((NX, NY, 8, 128), F32),
            pltpu.VMEM((NZ, 8, 128), F32),
            pltpu.VMEM((2 * NZ, 8, 128), F32),
            sem((5,)), sem((2 * SLOTS,)),
            sem((NY,)), sem((NY,)), sem((4,)), sem((4,)), sem, sem, sem((NZ,)), sem((NZ,)),
            sem((NX, NY)), sem((NX, NY)), sem((NX, NY)), sem((NX, NY)), sem((NX, NY)), sem((NX, NY)),
            sem((2 * NZ,)), sem((2 * NZ,)),
        ],
        compiler_params=pltpu.CompilerParams(
            collective_id=0, has_side_effects=True, vmem_limit_bytes=48 * 1024 * 1024
        ),
    )(*(pltpu.with_memory_space_constraint(a, pltpu.HBM) for a in args))


def solution(mesh):
    in_specs = (
        P(None, None, "seq"),
        P(None, None, "seq"),
        P(None, None, "seq"),
        P("rows", "seq", None),
        P("rows", "seq", None),
        P(),
        P(),
    )
    out_specs = P(None, None, "seq")
    return jax.shard_map(local, mesh=mesh, in_specs=in_specs, out_specs=out_specs, check_vma=False)
```

```python
import functools

import jax
import jax.numpy as jnp
from jax import lax
from jax.experimental import pallas as pl
from jax.experimental.pallas import tpu as pltpu
from jax.sharding import PartitionSpec as P

NX, NZ, NY = 4, 8, 4
HEAD_DIM = 128
SLOTS = 4
CTX = 256
NEG = -1e30
SCALE = HEAD_DIM**-0.5 * 1.4426950408889634
MESH = pl.DeviceIdType.MESH
F32, BF16, I32 = jnp.float32, jnp.bfloat16, jnp.int32


def iota(shape, dim):
    return lax.broadcasted_iota(I32, shape, dim)


def kernel(
    q_hbm, nk_hbm, nv_hbm, k_hbm, v_hbm, len_hbm, slot_hbm, out_ref,
    q_in, nk_in, nv_in, len_ref, slot_ref, k_buf, v_buf,
    new_y, new_z, new_tile, q_z, q_xy, o_xy, ml_xy, o_in, ml_in, fin, fin_in,
    in_sem, cache_sem,
    ny_s, ny_r, nz_s, nz_r, nc_s, nc_r, qz_s, qz_r, qxy_s, qxy_r, o_s, o_r, ml_s, ml_r, f_s, f_r,
):
    seq, core = lax.axis_index("seq"), lax.axis_index("rows")
    y = lax.rem(seq, NY)
    z = lax.rem(lax.div(seq, NY), NZ)
    x = lax.div(seq, NY * NZ)
    pair, half = lax.div(y, 2), lax.rem(y, 2)
    zq = lax.rem(z, 4)

    def at(xx, zz, yy, cc):
        return {"seq": (xx * NZ + zz) * NY + yy, "rows": cc}

    def remote(src, dst, send, recv, target):
        return pltpu.make_async_remote_copy(
            src_ref=src, dst_ref=dst, send_sem=send, recv_sem=recv, device_id=target, device_id_type=MESH
        )

    z_peer = [[at(x, lax.rem(z + d, NZ), y, c) for d in range(NZ)] for c in (core, 1 - core)]
    xy_peer = [[at(lax.rem(x + a, NX), z, lax.rem(y + b, NY), core) for b in range(NY)] for a in range(NX)]
    half_peer = [at(x, z - zq + lax.rem(zq + d, 4), y, core) for d in range(4)]
    others = [(a, b) for a in range(NX) for b in range(NY) if a or b]

    barrier = pltpu.get_barrier_semaphore()
    far = (4, 3, 5, 2, 6, 1, 7)
    peers = [z_peer[i][d] for d in far for i in (1, 0)] + [xy_peer[a][b] for a in (2, 1, 3, 0) for b in (2, 1, 3, 0) if a or b] + [z_peer[1][0]]
    for p in peers:
        pl.semaphore_signal(barrier, inc=1, device_id=p, device_id_type=MESH)

    loads = [
        pltpu.make_async_copy(q_hbm, q_in, in_sem.at[0]),
        pltpu.make_async_copy(slot_hbm, slot_ref, in_sem.at[1]),
        pltpu.make_async_copy(nk_hbm, nk_in, in_sem.at[2]),
        pltpu.make_async_copy(nv_hbm, nv_in, in_sem.at[3]),
        pltpu.make_async_copy(len_hbm, len_ref, in_sem.at[4]),
    ]
    for c in loads:
        c.start()

    k_loads = [pltpu.make_async_copy(k_hbm.at[s], k_buf.at[s], cache_sem.at[s]) for s in range(SLOTS)]
    v_loads = [pltpu.make_async_copy(v_hbm.at[s], v_buf.at[s], cache_sem.at[SLOTS + s]) for s in range(SLOTS)]
    for c in loads:
        c.wait()
    slots = [slot_ref[r] for r in range(8)]

    def by_slot(ref):
        width = ref.shape[2]
        row = iota((8, width), 0)
        wanted = core * SLOTS + lax.rem(row, 4)
        acc = jnp.zeros((8, width), F32)
        for t in range(2):
            whole = ref[t].astype(F32)
            for r in range(8):
                hit = (wanted == slots[r]) & (lax.div(row, 4) == t)
                acc = jnp.where(hit, jnp.broadcast_to(whole[r : r + 1], (8, width)), acc)
        return acc

    lane, row8 = iota((8, 128), 1), iota((8, 128), 0)
    mine = by_slot(q_in)
    q_z[z] = jnp.concatenate([mine[0:4], mine[4:8]], axis=1)

    pl.semaphore_wait(barrier, len(peers))

    def qz_copy(d, origin):
        return remote(q_z.at[origin], q_z.at[origin], qz_s.at[d], qz_r.at[d], z_peer[0][d])

    qz = [qz_copy(d, z) for d in (4, 3, 5, 2, 6, 1, 7)]
    for c in qz + k_loads + v_loads:
        c.start()

    base = zq * 32 + y * 8
    for i, ref in enumerate((nk_in, nv_in)):
        part = by_slot(ref)
        acc = jnp.zeros((8, 128), F32)
        for f in range(8):
            acc = jnp.where(lane == base + f, jnp.broadcast_to(part[:, f : f + 1], (8, 128)), acc)
        new_y[0, 8 * i : 8 * i + 8] = acc
    new_y[0, 16:24] = jnp.where(lax.div(lane, 64) == half, jnp.concatenate([mine, mine], axis=1), 0.0)
    ny = [remote(new_y.at[0], new_y.at[d], ny_s.at[d], ny_r.at[d], xy_peer[0][d]) for d in range(1, NY)]
    for c in ny:
        c.start()

    slot_of = lax.rem(iota((128, CTX), 0), SLOTS)
    limit = jnp.zeros((128, CTX), I32)
    for s in range(SLOTS):
        n = jnp.int32(0)
        for r in range(8):
            n = n + jnp.where(slots[r] == core * SLOTS + s, len_ref[r], 0)
        limit = jnp.where(slot_of == s, n, limit)
    valid = seq * CTX + iota((128, CTX), 1) < limit
    left16, left32 = iota((16, 128), 1) < 64, iota((32, 128), 1) < 64

    for d in range(1, NZ):
        qz_copy(d, lax.rem(z + NZ - d, NZ)).wait_recv()
    q_xy[x, y] = jnp.concatenate([q_z[i] for i in range(NZ)], axis=0).astype(BF16)

    def qxy_copy(a, b, xx, yy):
        return remote(q_xy.at[xx, yy], q_xy.at[xx, yy], qxy_s.at[a, b], qxy_r.at[a, b], xy_peer[a][b])

    qxy = [qxy_copy(a, b, x, y) for a in (2, 1, 3, 0) for b in (2, 1, 3, 0) if a or b]
    for c in qxy:
        c.start()

    for c in ny:
        c.wait_recv()
    new_z[0] = (new_y[0, 0:16] + new_y[1, 0:16]) + (new_y[2, 0:16] + new_y[3, 0:16])
    nz = [remote(new_z.at[0], new_z.at[d], nz_s.at[d], nz_r.at[d], half_peer[d]) for d in range(1, 4)]
    for c in nz:
        c.start()

    for c in k_loads + v_loads:
        c.wait()

    def attend(xb, slot):
        turned = []
        for hh in range(2):
            a, b = q_xy[xb, 2 * hh].astype(F32), q_xy[xb, 2 * hh + 1].astype(F32)
            turned.append(jnp.where(left32, a, pltpu.roll(b, 64, 1)).astype(BF16))
            turned.append(jnp.where(left32, pltpu.roll(a, 64, 1), b).astype(BF16))
        cols = pl.ds(pl.multiple_of(xb * 2 * HEAD_DIM, 2 * HEAD_DIM), 2 * HEAD_DIM)
        none = jnp.zeros((64, HEAD_DIM), BF16)
        q0, q1 = (jnp.concatenate([u[16 * j : 16 * j + 16] for u in turned], axis=0) for j in range(2))
        q = jnp.concatenate(
            [jnp.concatenate([q0, none], axis=1), jnp.concatenate([none, q1], axis=1)], axis=0
        )
        scores = None
        for s in range(SLOTS):
            part = lax.dot_general(q, k_buf[s, :, cols], (((1,), (1,)), ((), ())), preferred_element_type=F32)
            scores = part if s == 0 else jnp.where(slot_of == s, part, scores)
        scores = jnp.where(valid, scores * SCALE, NEG)
        top = jnp.maximum(jnp.max(scores, axis=1, keepdims=True), NEG / 2)
        p = jnp.exp2(scores - top)
        total = jnp.sum(p, axis=1, keepdims=True)
        p = p.astype(BF16)
        sums = None
        for s in range(SLOTS):
            part = jnp.dot(p, v_buf[s, :, cols], preferred_element_type=F32)
            sums = part if s == 0 else jnp.where(slot_of == s, part, sums)
        ml = jnp.zeros((8, 128), F32)
        for j in range(2):
            out = sums[64 * j : 64 * j + 64, HEAD_DIM * j : HEAD_DIM * j + HEAD_DIM]
            for hh in range(2):
                first, second = out[32 * hh : 32 * hh + 16], out[32 * hh + 16 : 32 * hh + 32]
                rows = slice(16 * j, 16 * j + 16)
                o_xy[slot, 2 * hh, rows] = jnp.where(left16, first, pltpu.roll(second, 64, 1)).astype(BF16)
                o_xy[slot, 2 * hh + 1, rows] = jnp.where(left16, pltpu.roll(first, 64, 1), second).astype(BF16)
                for t in range(2):
                    for rh in range(2):
                        start = 64 * j + 32 * hh + 16 * t + 8 * rh
                        here = slice(start, start + 8)
                        i = hh * 8 + j * 4 + t * 2 + rh
                        ml = jnp.where(lane == i, top[here], ml)
                        ml = jnp.where(lane == 64 + i, total[here], ml)
        ml_xy[slot] = ml

    back = {}
    for a in range(NX):
        xb = lax.rem(x + NX - a, NX)
        for b in range(NY):
            if a or b:
                qxy_copy(a, b, xb, lax.rem(y + NY - b, NY)).wait_recv()
        attend(xb, a)
        for b in (2, 1, 3, 0):
            if a or b:
                target = xy_peer[(NX - a) % NX][b]
                yy = lax.rem(y + b, NY)
                back[a, b] = (
                    remote(ml_xy.at[a], ml_in.at[a, b], ml_s.at[a, b], ml_r.at[a, b], target),
                    remote(o_xy.at[a, yy], o_in.at[a, b], o_s.at[a, b], o_r.at[a, b], target),
                )
                for c in back[a, b]:
                    c.start()

    for c in nz:
        c.wait_recv()
    new = (new_z[0] + new_z[1]) + (new_z[2] + new_z[3])

    def spread(block):
        turned = jnp.concatenate([block[4:8], block[0:4]], axis=0)
        return jnp.where(row8 < 4, block, turned), jnp.where(row8 < 4, turned, block)

    key0, key1 = spread(new[0:8])
    val0, val1 = spread(new[8:16])
    qf = new_y[0, 16:24] + jnp.where(half == 0, new_y[3, 16:24], new_y[1, 16:24])
    second = iota((8, 1), 0) >= 4
    s0 = jnp.sum(qf * key0, axis=1, keepdims=True) * SCALE
    s1 = jnp.where(second, jnp.sum(qf * key1, axis=1, keepdims=True) * SCALE, NEG)
    new_top = jnp.maximum(s0, s1)
    p0 = jnp.exp2(s0 - new_top)
    p1 = jnp.where(second, jnp.exp2(s1 - new_top), 0.0)
    new_total = p0 + p1
    new_out = p0 * val0 + p1 * val1
    new_out = jnp.where(half == 0, new_out, pltpu.roll(new_out, 64, 1))
    new_tile[0] = jnp.where(lane < 64, new_out, jnp.where(lane < 96, new_top, new_total))
    nc = remote(new_tile.at[0], new_tile.at[1], nc_s, nc_r, z_peer[1][0])
    nc.start()

    def by_lane(tile, i):
        return jnp.where(lane < 64, tile[:, i : i + 1], tile[:, i + 2 : i + 3])

    def gathered(group):
        keys = [(a, b) for a in group for b in range(NY)]
        for i in range(2):
            for key in keys:
                if key in back:
                    back[key][i].wait_recv()
        mls = [ml_in[a, b] if a or b else ml_xy[0] for a, b in keys]
        mls = [jnp.where(pair == 0, m, pltpu.roll(m, 120, 1)) for m in mls]
        outs = [o_in.at[a, b] if a or b else o_xy.at[0, y] for a, b in keys]
        top = functools.reduce(jnp.maximum, mls)
        factors = [jnp.exp2(m - top) for m in mls]
        total = sum(pltpu.roll(f, 64, 1) * m for f, m in zip(factors, mls))
        sums = []
        for j in range(2):
            rows = [o[16 * j : 16 * j + 16].astype(F32) for o in outs]
            for rh in range(2):
                sums.append(sum(by_lane(f, j * 4 + rh) * o[8 * rh : 8 * rh + 8] for f, o in zip(factors, rows)))
        return top, total, sums

    early, late = gathered((0, 1)), gathered((2, 3))
    top = jnp.maximum(early[0], late[0])
    factors = [jnp.exp2(g[0] - top) for g in (early, late)]
    total = sum(pltpu.roll(f, 64, 1) * g[1] for f, g in zip(factors, (early, late)))
    for j in range(2):
        for rh in range(2):
            i = j * 4 + rh
            acc = sum(by_lane(f, i) * g[2][2 * j + rh] for f, g in zip(factors, (early, late)))
            swapped = pltpu.roll(acc, 64, 1)
            ends = [jnp.where(lane < 96, top[:, k : k + 1], total[:, 64 + k : 65 + k]) for k in (i, i + 2)]
            low = jnp.where(lane < 64, acc, ends[0])
            high = jnp.where(lane < 64, swapped, ends[1])
            zz = j * 4 + rh * 2
            fin[zz] = jnp.where(row8 < 4, low, pltpu.roll(high, 4, 0))
            fin[zz + 1] = jnp.where(row8 < 4, pltpu.roll(low, 4, 0), high)

    f = []
    for d in (4, 3, 5, 2, 6, 1, 7, 0):
        for other in (1, 0):
            if d or other:
                i = other * NZ + d
                f.append(remote(fin.at[lax.rem(z + d, NZ)], fin_in.at[i], f_s.at[i], f_r.at[i], z_peer[other][d]))
                f[-1].start()
    row = iota((8, 64), 0)
    slot_row = jnp.zeros((8, 64), I32)
    for r in range(8):
        slot_row = jnp.where(row == r, slots[r], slot_row)
    for c in [nc] + ny + nz + qz + qxy + [c for pairs in back.values() for c in pairs]:
        c.wait_send()
    for c in [nc] + f:
        c.wait_recv()

    parts = []
    for other in range(2):
        tiles = [fin_in[other * NZ + d] if d or other else fin[z] for d in range(NZ)] + [new_tile[other]]
        top = functools.reduce(jnp.maximum, tiles)
        acc = sum(jnp.exp2(t - top)[:, 64:65] * t for t in tiles)
        parts.append(acc[:, :64] / acc[:, 96:97])
    for t in range(2):
        result = jnp.zeros((8, 64), F32)
        for other in range(2):
            group = core + other - 2 * core * other
            for s in range(SLOTS):
                i = t * 4 + s
                found = slot_row == group * SLOTS + s
                result = jnp.where(found, jnp.broadcast_to(parts[other][i : i + 1], (8, 64)), result)
        out_ref[t] = result.astype(BF16)

    for c in f:
        c.wait_send()


def local(queries, new_keys, new_values, key_cache, value_cache, lengths, row_slot):
    sem = pltpu.SemaphoreType.DMA
    args = (queries, new_keys, new_values, key_cache, value_cache, lengths, row_slot)
    return pl.pallas_call(
        kernel,
        out_shape=jax.ShapeDtypeStruct(queries.shape, BF16),
        in_specs=[pl.BlockSpec(memory_space=pltpu.HBM)] * 7,
        out_specs=pl.BlockSpec(memory_space=pltpu.VMEM),
        scratch_shapes=[
            pltpu.VMEM(queries.shape, BF16),
            pltpu.VMEM(new_keys.shape, BF16),
            pltpu.VMEM(new_values.shape, BF16),
            pltpu.SMEM(lengths.shape, I32),
            pltpu.SMEM(row_slot.shape, I32),
            pltpu.VMEM(key_cache.shape, BF16),
            pltpu.VMEM(value_cache.shape, BF16),
            pltpu.VMEM((NY, 24, 128), F32),
            pltpu.VMEM((4, 16, 128), F32),
            pltpu.VMEM((2, 8, 128), F32),
            pltpu.VMEM((NZ, 4, 128), F32),
            pltpu.VMEM((NX, NY, 32, 128), BF16),
            pltpu.VMEM((NX, NY, 32, 128), BF16),
            pltpu.VMEM((NX, 8, 128), F32),
            pltpu.VMEM((NX, NY, 32, 128), BF16),
            pltpu.VMEM((NX, NY, 8, 128), F32),
            pltpu.VMEM((NZ, 8, 128), F32),
            pltpu.VMEM((2 * NZ, 8, 128), F32),
            sem((5,)), sem((2 * SLOTS,)),
            sem((NY,)), sem((NY,)), sem((4,)), sem((4,)), sem, sem, sem((NZ,)), sem((NZ,)),
            sem((NX, NY)), sem((NX, NY)), sem((NX, NY)), sem((NX, NY)), sem((NX, NY)), sem((NX, NY)),
            sem((2 * NZ,)), sem((2 * NZ,)),
        ],
        compiler_params=pltpu.CompilerParams(
            collective_id=0, has_side_effects=True, vmem_limit_bytes=48 * 1024 * 1024
        ),
    )(*(pltpu.with_memory_space_constraint(a, pltpu.HBM) for a in args))


def solution(mesh):
    in_specs = (
        P(None, None, "seq"),
        P(None, None, "seq"),
        P(None, None, "seq"),
        P("rows", "seq", None),
        P("rows", "seq", None),
        P(),
        P(),
    )
    out_specs = P(None, None, "seq")
    return jax.shard_map(local, mesh=mesh, in_specs=in_specs, out_specs=out_specs, check_vma=False)
```

```python
import functools

import jax
import jax.numpy as jnp
from jax import lax
from jax.experimental import pallas as pl
from jax.experimental.pallas import tpu as pltpu
from jax.sharding import PartitionSpec as P

NX, NZ, NY = 4, 8, 4
HEAD_DIM = 128
SLOTS = 4
CTX = 256
NEG = -1e30
SCALE = HEAD_DIM**-0.5 * 1.4426950408889634
MESH = pl.DeviceIdType.MESH
F32, BF16, I32 = jnp.float32, jnp.bfloat16, jnp.int32


def iota(shape, dim):
    return lax.broadcasted_iota(I32, shape, dim)


def kernel(
    q_hbm, nk_hbm, nv_hbm, k_hbm, v_hbm, len_hbm, slot_hbm, out_ref,
    q_in, nk_in, nv_in, len_ref, slot_ref, k_buf, v_buf,
    new_y, new_z, new_tile, q_z, q_xy, o_xy, ml_xy, o_in, ml_in, fin, fin_in,
    in_sem, cache_sem,
    ny_s, ny_r, nz_s, nz_r, nc_s, nc_r, qz_s, qz_r, qxy_s, qxy_r, o_s, o_r, ml_s, ml_r, f_s, f_r,
):
    seq, core = lax.axis_index("seq"), lax.axis_index("rows")
    y = lax.rem(seq, NY)
    z = lax.rem(lax.div(seq, NY), NZ)
    x = lax.div(seq, NY * NZ)
    pair, half = lax.div(y, 2), lax.rem(y, 2)
    zq = lax.rem(z, 4)

    def at(xx, zz, yy, cc):
        return {"seq": (xx * NZ + zz) * NY + yy, "rows": cc}

    def remote(src, dst, send, recv, target):
        return pltpu.make_async_remote_copy(
            src_ref=src, dst_ref=dst, send_sem=send, recv_sem=recv, device_id=target, device_id_type=MESH
        )

    z_peer = [[at(x, lax.rem(z + d, NZ), y, c) for d in range(NZ)] for c in (core, 1 - core)]
    xy_peer = [[at(lax.rem(x + a, NX), z, lax.rem(y + b, NY), core) for b in range(NY)] for a in range(NX)]
    half_peer = [at(x, z - zq + lax.rem(zq + d, 4), y, core) for d in range(4)]
    others = [(a, b) for a in range(NX) for b in range(NY) if a or b]

    barrier = pltpu.get_barrier_semaphore()
    far = (4, 3, 5, 2, 6, 1, 7)
    peers = [z_peer[i][d] for d in far for i in (1, 0)] + [xy_peer[a][b] for a in (2, 1, 3, 0) for b in (2, 1, 3, 0) if a or b] + [z_peer[1][0]]
    for p in peers:
        pl.semaphore_signal(barrier, inc=1, device_id=p, device_id_type=MESH)

    loads = [
        pltpu.make_async_copy(q_hbm, q_in, in_sem.at[0]),
        pltpu.make_async_copy(slot_hbm, slot_ref, in_sem.at[1]),
        pltpu.make_async_copy(nk_hbm, nk_in, in_sem.at[2]),
        pltpu.make_async_copy(nv_hbm, nv_in, in_sem.at[3]),
        pltpu.make_async_copy(len_hbm, len_ref, in_sem.at[4]),
    ]
    for c in loads:
        c.start()

    k_loads = [pltpu.make_async_copy(k_hbm.at[s], k_buf.at[s], cache_sem.at[s]) for s in range(SLOTS)]
    v_loads = [pltpu.make_async_copy(v_hbm.at[s], v_buf.at[s], cache_sem.at[SLOTS + s]) for s in range(SLOTS)]
    for c in loads:
        c.wait()
    slots = [slot_ref[r] for r in range(8)]

    def by_slot(ref):
        width = ref.shape[2]
        row = iota((8, width), 0)
        wanted = core * SLOTS + lax.rem(row, 4)
        acc = jnp.zeros((8, width), F32)
        for t in range(2):
            whole = ref[t].astype(F32)
            for r in range(8):
                hit = (wanted == slots[r]) & (lax.div(row, 4) == t)
                acc = jnp.where(hit, jnp.broadcast_to(whole[r : r + 1], (8, width)), acc)
        return acc

    lane, row8 = iota((8, 128), 1), iota((8, 128), 0)
    mine = by_slot(q_in)
    q_z[z] = jnp.concatenate([mine[0:4], mine[4:8]], axis=1)

    pl.semaphore_wait(barrier, len(peers))

    def qz_copy(d, origin):
        return remote(q_z.at[origin], q_z.at[origin], qz_s.at[d], qz_r.at[d], z_peer[0][d])

    qz = [qz_copy(d, z) for d in (4, 3, 5, 2, 6, 1, 7)]
    for c in qz + k_loads + v_loads:
        c.start()

    base = zq * 32 + y * 8
    for i, ref in enumerate((nk_in, nv_in)):
        part = by_slot(ref)
        acc = jnp.zeros((8, 128), F32)
        for f in range(8):
            acc = jnp.where(lane == base + f, jnp.broadcast_to(part[:, f : f + 1], (8, 128)), acc)
        new_y[0, 8 * i : 8 * i + 8] = acc
    new_y[0, 16:24] = jnp.where(lax.div(lane, 64) == half, jnp.concatenate([mine, mine], axis=1), 0.0)
    ny = [remote(new_y.at[0], new_y.at[d], ny_s.at[d], ny_r.at[d], xy_peer[0][d]) for d in range(1, NY)]
    for c in ny:
        c.start()

    slot_of = lax.rem(iota((128, CTX), 0), SLOTS)
    limit = jnp.zeros((128, CTX), I32)
    for s in range(SLOTS):
        n = jnp.int32(0)
        for r in range(8):
            n = n + jnp.where(slots[r] == core * SLOTS + s, len_ref[r], 0)
        limit = jnp.where(slot_of == s, n, limit)
    valid = seq * CTX + iota((128, CTX), 1) < limit
    left16, left32 = iota((16, 128), 1) < 64, iota((32, 128), 1) < 64

    for d in range(1, NZ):
        qz_copy(d, lax.rem(z + NZ - d, NZ)).wait_recv()
    q_xy[x, y] = jnp.concatenate([q_z[i] for i in range(NZ)], axis=0).astype(BF16)

    def qxy_copy(a, b, xx, yy):
        return remote(q_xy.at[xx, yy], q_xy.at[xx, yy], qxy_s.at[a, b], qxy_r.at[a, b], xy_peer[a][b])

    qxy = [qxy_copy(a, b, x, y) for a in (2, 1, 3, 0) for b in (2, 1, 3, 0) if a or b]
    for c in qxy:
        c.start()

    for c in ny:
        c.wait_recv()
    new_z[0] = (new_y[0, 0:16] + new_y[1, 0:16]) + (new_y[2, 0:16] + new_y[3, 0:16])
    nz = [remote(new_z.at[0], new_z.at[d], nz_s.at[d], nz_r.at[d], half_peer[d]) for d in range(1, 4)]
    for c in nz:
        c.start()

    for c in k_loads + v_loads:
        c.wait()

    def attend(xb, slot):
        turned = []
        for hh in range(2):
            a, b = q_xy[xb, 2 * hh].astype(F32), q_xy[xb, 2 * hh + 1].astype(F32)
            turned.append(jnp.where(left32, a, pltpu.roll(b, 64, 1)).astype(BF16))
            turned.append(jnp.where(left32, pltpu.roll(a, 64, 1), b).astype(BF16))
        cols = pl.ds(pl.multiple_of(xb * 2 * HEAD_DIM, 2 * HEAD_DIM), 2 * HEAD_DIM)
        none = jnp.zeros((64, HEAD_DIM), BF16)
        q0, q1 = (jnp.concatenate([u[16 * j : 16 * j + 16] for u in turned], axis=0) for j in range(2))
        q = jnp.concatenate(
            [jnp.concatenate([q0, none], axis=1), jnp.concatenate([none, q1], axis=1)], axis=0
        )
        scores = None
        for s in range(SLOTS):
            part = lax.dot_general(q, k_buf[s, :, cols], (((1,), (1,)), ((), ())), preferred_element_type=F32)
            scores = part if s == 0 else jnp.where(slot_of == s, part, scores)
        scores = jnp.where(valid, scores * SCALE, NEG)
        top = jnp.maximum(jnp.max(scores, axis=1, keepdims=True), NEG / 2)
        p = jnp.exp2(scores - top)
        total = jnp.sum(p, axis=1, keepdims=True)
        p = p.astype(BF16)
        sums = None
        for s in range(SLOTS):
            part = jnp.dot(p, v_buf[s, :, cols], preferred_element_type=F32)
            sums = part if s == 0 else jnp.where(slot_of == s, part, sums)
        ml = [jnp.zeros((8, 128), F32)] * 2
        for j in range(2):
            out = sums[64 * j : 64 * j + 64, HEAD_DIM * j : HEAD_DIM * j + HEAD_DIM]
            for hh in range(2):
                first, second = out[32 * hh : 32 * hh + 16], out[32 * hh + 16 : 32 * hh + 32]
                rows = slice(16 * j, 16 * j + 16)
                o_xy[slot, 2 * hh, rows] = jnp.where(left16, first, pltpu.roll(second, 64, 1)).astype(BF16)
                o_xy[slot, 2 * hh + 1, rows] = jnp.where(left16, pltpu.roll(first, 64, 1), second).astype(BF16)
                for t in range(2):
                    for rh in range(2):
                        start = 64 * j + 32 * hh + 16 * t + 8 * rh
                        here = slice(start, start + 8)
                        i = j * 4 + t * 2 + rh
                        ml[hh] = jnp.where(lane == i, top[here], ml[hh])
                        ml[hh] = jnp.where(lane == 64 + i, total[here], ml[hh])
        ml_xy[slot, 0], ml_xy[slot, 1] = ml

    back = {}
    for a in range(NX):
        xb = lax.rem(x + NX - a, NX)
        for b in range(NY):
            if a or b:
                qxy_copy(a, b, xb, lax.rem(y + NY - b, NY)).wait_recv()
        attend(xb, a)
        for b in (2, 1, 3, 0):
            if a or b:
                target = xy_peer[(NX - a) % NX][b]
                yy = lax.rem(y + b, NY)
                back[a, b] = (
                    remote(ml_xy.at[a, lax.div(yy, 2)], ml_in.at[a, b], ml_s.at[a, b], ml_r.at[a, b], target),
                    remote(o_xy.at[a, yy], o_in.at[a, b], o_s.at[a, b], o_r.at[a, b], target),
                )
                for c in back[a, b]:
                    c.start()

    for c in nz:
        c.wait_recv()
    new = (new_z[0] + new_z[1]) + (new_z[2] + new_z[3])

    def spread(block):
        turned = jnp.concatenate([block[4:8], block[0:4]], axis=0)
        return jnp.where(row8 < 4, block, turned), jnp.where(row8 < 4, turned, block)

    key0, key1 = spread(new[0:8])
    val0, val1 = spread(new[8:16])
    qf = new_y[0, 16:24] + jnp.where(half == 0, new_y[3, 16:24], new_y[1, 16:24])
    second = iota((8, 1), 0) >= 4
    s0 = jnp.sum(qf * key0, axis=1, keepdims=True) * SCALE
    s1 = jnp.where(second, jnp.sum(qf * key1, axis=1, keepdims=True) * SCALE, NEG)
    new_top = jnp.maximum(s0, s1)
    p0 = jnp.exp2(s0 - new_top)
    p1 = jnp.where(second, jnp.exp2(s1 - new_top), 0.0)
    new_total = p0 + p1
    new_out = p0 * val0 + p1 * val1
    new_out = jnp.where(half == 0, new_out, pltpu.roll(new_out, 64, 1))
    new_tile[0] = jnp.where(lane < 64, new_out, jnp.where(lane < 96, new_top, new_total))
    nc = remote(new_tile.at[0], new_tile.at[1], nc_s, nc_r, z_peer[1][0])
    nc.start()

    def by_lane(tile, i):
        return jnp.where(lane < 64, tile[:, i : i + 1], tile[:, i + 2 : i + 3])

    def gathered(group):
        keys = [(a, b) for a in group for b in range(NY)]
        for i in range(2):
            for key in keys:
                if key in back:
                    back[key][i].wait_recv()
        mls = [ml_in[a, b] if a or b else ml_xy[0, pair] for a, b in keys]
        outs = [o_in.at[a, b] if a or b else o_xy.at[0, y] for a, b in keys]
        top = functools.reduce(jnp.maximum, mls)
        factors = [jnp.exp2(m - top) for m in mls]
        total = sum(pltpu.roll(f, 64, 1) * m for f, m in zip(factors, mls))
        sums = []
        for j in range(2):
            rows = [o[16 * j : 16 * j + 16].astype(F32) for o in outs]
            for rh in range(2):
                sums.append(sum(by_lane(f, j * 4 + rh) * o[8 * rh : 8 * rh + 8] for f, o in zip(factors, rows)))
        return top, total, sums

    early, late = gathered((0, 1)), gathered((2, 3))
    top = jnp.maximum(early[0], late[0])
    factors = [jnp.exp2(g[0] - top) for g in (early, late)]
    total = sum(pltpu.roll(f, 64, 1) * g[1] for f, g in zip(factors, (early, late)))
    for j in range(2):
        for rh in range(2):
            i = j * 4 + rh
            acc = sum(by_lane(f, i) * g[2][2 * j + rh] for f, g in zip(factors, (early, late)))
            swapped = pltpu.roll(acc, 64, 1)
            ends = [jnp.where(lane < 96, top[:, k : k + 1], total[:, 64 + k : 65 + k]) for k in (i, i + 2)]
            low = jnp.where(lane < 64, acc, ends[0])
            high = jnp.where(lane < 64, swapped, ends[1])
            zz = j * 4 + rh * 2
            fin[zz] = jnp.where(row8 < 4, low, pltpu.roll(high, 4, 0))
            fin[zz + 1] = jnp.where(row8 < 4, pltpu.roll(low, 4, 0), high)

    f = []
    for d in (4, 3, 5, 2, 6, 1, 7, 0):
        for other in (1, 0):
            if d or other:
                i = other * NZ + d
                f.append(remote(fin.at[lax.rem(z + d, NZ)], fin_in.at[i], f_s.at[i], f_r.at[i], z_peer[other][d]))
                f[-1].start()
    row = iota((8, 64), 0)
    slot_row = jnp.zeros((8, 64), I32)
    for r in range(8):
        slot_row = jnp.where(row == r, slots[r], slot_row)
    for c in [nc] + ny + nz + qz + qxy + [c for pairs in back.values() for c in pairs]:
        c.wait_send()
    for c in [nc] + f:
        c.wait_recv()

    parts = []
    for other in range(2):
        tiles = [fin_in[other * NZ + d] if d or other else fin[z] for d in range(NZ)] + [new_tile[other]]
        top = functools.reduce(jnp.maximum, tiles)
        acc = sum(jnp.exp2(t - top)[:, 64:65] * t for t in tiles)
        parts.append(acc[:, :64] / acc[:, 96:97])
    for t in range(2):
        result = jnp.zeros((8, 64), F32)
        for other in range(2):
            group = core + other - 2 * core * other
            for s in range(SLOTS):
                i = t * 4 + s
                found = slot_row == group * SLOTS + s
                result = jnp.where(found, jnp.broadcast_to(parts[other][i : i + 1], (8, 64)), result)
        out_ref[t] = result.astype(BF16)

    for c in f:
        c.wait_send()


def local(queries, new_keys, new_values, key_cache, value_cache, lengths, row_slot):
    sem = pltpu.SemaphoreType.DMA
    args = (queries, new_keys, new_values, key_cache, value_cache, lengths, row_slot)
    return pl.pallas_call(
        kernel,
        out_shape=jax.ShapeDtypeStruct(queries.shape, BF16),
        in_specs=[pl.BlockSpec(memory_space=pltpu.HBM)] * 7,
        out_specs=pl.BlockSpec(memory_space=pltpu.VMEM),
        scratch_shapes=[
            pltpu.VMEM(queries.shape, BF16),
            pltpu.VMEM(new_keys.shape, BF16),
            pltpu.VMEM(new_values.shape, BF16),
            pltpu.SMEM(lengths.shape, I32),
            pltpu.SMEM(row_slot.shape, I32),
            pltpu.VMEM(key_cache.shape, BF16),
            pltpu.VMEM(value_cache.shape, BF16),
            pltpu.VMEM((NY, 24, 128), F32),
            pltpu.VMEM((4, 16, 128), F32),
            pltpu.VMEM((2, 8, 128), F32),
            pltpu.VMEM((NZ, 4, 128), F32),
            pltpu.VMEM((NX, NY, 32, 128), BF16),
            pltpu.VMEM((NX, NY, 32, 128), BF16),
            pltpu.VMEM((NX, 2, 8, 128), F32),
            pltpu.VMEM((NX, NY, 32, 128), BF16),
            pltpu.VMEM((NX, NY, 8, 128), F32),
            pltpu.VMEM((NZ, 8, 128), F32),
            pltpu.VMEM((2 * NZ, 8, 128), F32),
            sem((5,)), sem((2 * SLOTS,)),
            sem((NY,)), sem((NY,)), sem((4,)), sem((4,)), sem, sem, sem((NZ,)), sem((NZ,)),
            sem((NX, NY)), sem((NX, NY)), sem((NX, NY)), sem((NX, NY)), sem((NX, NY)), sem((NX, NY)),
            sem((2 * NZ,)), sem((2 * NZ,)),
        ],
        compiler_params=pltpu.CompilerParams(
            collective_id=0, has_side_effects=True, vmem_limit_bytes=48 * 1024 * 1024
        ),
    )(*(pltpu.with_memory_space_constraint(a, pltpu.HBM) for a in args))


def solution(mesh):
    in_specs = (
        P(None, None, "seq"),
        P(None, None, "seq"),
        P(None, None, "seq"),
        P("rows", "seq", None),
        P("rows", "seq", None),
        P(),
        P(),
    )
    out_specs = P(None, None, "seq")
    return jax.shard_map(local, mesh=mesh, in_specs=in_specs, out_specs=out_specs, check_vma=False)
```
